32 devices in a mesh: ctx: 16 (over z, x, core), head: 2 (over y).
Axes of the slice: x: 2, y: 2, z: 4, core: 2. Of those that a mesh axis runs over, the one named last changes fastest.
Arguments:
- q_nope: bfloat16 [4096, 16, 128], P('ctx', 'head'), may hold values from -6 to 6
- q_rope: bfloat16 [4096, 16, 64], P('ctx', 'head'), may hold values from -300 to 300
- c_kv: bfloat16 [4096, 512], P('ctx'), may hold values from -6 to 6
- k_rope: bfloat16 [4096, 64], P('ctx'), may hold values from -6 to 6
- block_pos: int32 [32], replicated, may hold values from 0 to 31, as said below
- w_uk: bfloat16 [16, 128, 512], P('head'), may hold values from -0.5 to 0.5
- w_uv: bfloat16 [16, 512, 128], P('head'), may hold values from -6 to 6
Outputs:
- attn_out: bfloat16 [4096, 16, 128], P('ctx', 'head')
The draws below stay inside these ranges and needn't reach their ends.
Inputs may be any that keep to these rules, and one draw needn't show every extreme that they name: block_pos is the mirrored-pair order turned by some c: block_pos[2 s] = (s + c) mod 16 and block_pos[2 s + 1] = 31 - block_pos[2 s].
All inputs are finite; a program needn't handle non-finite values.
Results may differ from the reference program's by a relative error of at most 0.0072.
Values may be sent and summed in bfloat16 or wider, within the bound.
A program may use at most 64 MiB of HBM per device.

```python
import math
import jax
import jax.numpy as jnp
from jax import lax

LAT = 512
ROPE = 64
NOPE = 128
VDIM = 128
H = 16
BLK = 128
TOKENS = 4096
N_CTX = 16


def rope_pair(key, strength):
    base_k = jnp.clip(jax.random.normal(jax.random.fold_in(key, 101), (TOKENS, ROPE), jnp.float32), -5.0, 5.0)
    base_q = jnp.clip(jax.random.normal(jax.random.fold_in(key, 102), (TOKENS, H, ROPE), jnp.float32), -5.0, 5.0)
    row_ids = jnp.arange(TOKENS)
    active = strength > 0
    leader = (row_ids % 16 == 9) & active
    trailer = (row_ids % 16 == 8) & active
    keys = jnp.where(trailer[:, None], jnp.roll(base_k, -1, axis=0) * 1.012, base_k)
    factor = strength * (1.0 + 0.6 * (jnp.arange(H) % 3).astype(jnp.float32))
    queries = jnp.where(leader[:, None, None], factor[None, :, None] * keys[:, None, :], base_q)
    return (queries, keys)


def draw_q_rope(key, part):
    strength = 0.0
    queries, keys = rope_pair(key, strength)
    return queries.astype(jnp.bfloat16)


def draw_k_rope(key, part):
    strength = 0.0
    queries, keys = rope_pair(key, strength)
    return keys.astype(jnp.bfloat16)


def draw_block_pos(key, part):
    key = jax.random.fold_in(key, 7)
    turn = jax.random.randint(key, (), 0, N_CTX, dtype=jnp.int32)
    first = (jnp.arange(N_CTX, dtype=jnp.int32) + turn) % N_CTX
    second = 2 * N_CTX - 1 - first
    return jnp.stack([first, second], axis=1).reshape(-1).astype(jnp.int32)


def shard_levels(key, shape, shards, smallest, top_value):
    loudness, own = 1.0, jax.random.fold_in(key, 6)
    for axis_at, parts in shards:
        heights = jnp.exp(jax.random.uniform(jax.random.fold_in(own, axis_at), (parts,), jnp.float32, smallest / len(shards), top_value / len(shards)))
        loudness = loudness * jnp.repeat(heights, shape[axis_at] // parts).reshape([-1 if axis == axis_at else 1 for axis in range(len(shape))])
    return loudness


def bell_draw(rng, dims, width, limit, shards=(), held_as=jnp.bfloat16):
    level = shard_levels(rng, dims, shards, -0.22, 0.18) if shards else 1.0
    entries = jax.random.normal(rng, dims, jnp.float32) * width * level
    return jnp.minimum(jnp.maximum(entries, -limit), limit).astype(held_as)


def setup_inputs(seed: int = 0) -> dict:
    key_of = jax.random.split(jax.random.key(seed), 8)
    return {
        "q_nope": bell_draw(key_of[0], (TOKENS, H, NOPE), 1.0, 6.0, ((0, 16), (1, 2))),
        "q_rope": draw_q_rope(jax.random.fold_in(key_of[7], 71), 0),
        "c_kv": bell_draw(key_of[2], (TOKENS, LAT), 1.0, 6.0, ((0, 16),)),
        "k_rope": draw_k_rope(jax.random.fold_in(key_of[7], 71), 0),
        "block_pos": draw_block_pos(jax.random.fold_in(key_of[7], 71), 0),
        "w_uk": bell_draw(key_of[5], (H, NOPE, LAT), NOPE ** -0.5, 0.5, ((0, 2),)),
        "w_uv": bell_draw(key_of[6], (H, LAT, VDIM), 1.0, 6.0, ((0, 2),)),
    }


def reference(q_nope, q_rope, c_kv, k_rope, block_pos, w_uk, w_uv):
    rows = 2 * BLK
    scale = 1.0 / math.sqrt(NOPE + ROPE)
    span = jnp.arange(BLK, dtype=jnp.int32)
    uk_full = w_uk.astype(jnp.float32)
    uv_full = w_uv.astype(jnp.float32)

    def positions(source):
        pair = lax.dynamic_slice_in_dim(block_pos, (2 * source).astype(jnp.int32), 2)
        return (pair[:, None] * BLK + span[None, :]).reshape(-1)

    def one_shard(place):
        start = (place * rows).astype(jnp.int32)
        nope_rows = lax.dynamic_slice_in_dim(q_nope, start, rows, 0).astype(jnp.float32)
        rope_rows = lax.dynamic_slice_in_dim(q_rope, start, rows, 0).astype(jnp.float32)
        q_lat = jnp.einsum('thn,hnl->thl', nope_rows, uk_full).astype(jnp.bfloat16)
        q_lat = lax.optimization_barrier(q_lat).astype(jnp.float32)
        latents = []
        ropes = []
        key_pos = []
        for offset in (0, 1, -1, 2, -2):
            source = ((place - offset) % N_CTX).astype(jnp.int32)
            first = (source * rows).astype(jnp.int32)
            latents.append(lax.dynamic_slice_in_dim(c_kv, first, rows, 0))
            ropes.append(lax.dynamic_slice_in_dim(k_rope, first, rows, 0))
            key_pos.append(positions(source))
        latent = jnp.concatenate(latents, axis=0).astype(jnp.float32)
        rotary = jnp.concatenate(ropes, axis=0).astype(jnp.float32)
        kpos = jnp.concatenate(key_pos, axis=0)
        qpos = positions(place.astype(jnp.int32))
        score = (jnp.einsum('thl,kl->thk', q_lat, latent) + jnp.einsum('thr,kr->thk', rope_rows, rotary)) * scale
        visible = kpos[None, None, :] <= qpos[:, None, None]
        score = jnp.where(visible, score, -1e+30)
        top = lax.optimization_barrier(jnp.max(score, axis=2, keepdims=True))
        expo = jnp.where(visible, jnp.exp(score - top), 0.0)
        total = lax.optimization_barrier(jnp.sum(expo, axis=2))
        weights = lax.optimization_barrier(expo.astype(jnp.bfloat16)).astype(jnp.float32)
        o_lat = jnp.einsum('thk,kl->thl', weights, latent) / total[:, :, None]
        o_lat = lax.optimization_barrier(o_lat.astype(jnp.bfloat16)).astype(jnp.float32)
        return jnp.einsum('thl,hlv->thv', o_lat, uv_full).astype(jnp.bfloat16)
    blocks = lax.map(one_shard, jnp.arange(N_CTX, dtype=jnp.int32))
    return blocks.reshape(TOKENS, H, VDIM)
```

```python
import functools
import math

import jax
import jax.numpy as jnp
from jax import lax
from jax.experimental import pallas as pl
from jax.experimental.pallas import tpu as pltpu
from jax.sharding import PartitionSpec as P

MESH = pl.DeviceIdType.MESH
LANES = 128
PIECES = ((0, 5), (5, 4))
PARTNER, NEAR, FAR, WIDE = 0, 1, 2, 3


def nt_dot(a, b):
    return lax.dot_general(a, b, (((1,), (1,)), ((), ())), preferred_element_type=jnp.float32)


def attention_kernel(
    factor,
    pos_ref, ckv_ref, krope_ref, qn_hbm, qr_hbm, wuk_hbm, wuv_hbm, out_ref,
    qn, qr, wuk, wuv, flat, flat_rope, qs, held, keys, acc, top_s, sum_s,
    load_sem, send_sem, recv_sem,
):
    n = lax.axis_size("ctx")
    me = lax.axis_index("ctx")
    heads = qn.shape[1]
    blk = ckv_ref.shape[0] // 2
    lat = ckv_ref.shape[1]
    rope = krope_ref.shape[1]
    odd = lax.rem(me, 2)

    def at(by):
        return lax.rem(me + by + n, n)

    partner = at(1 - 2 * odd)
    near = at(2 * odd - 1)
    far = at(4 * odd - 2)
    wide = at(2 - 4 * odd)

    loads = [
        pltpu.make_async_copy(a, b, load_sem.at[i])
        for i, (a, b) in enumerate(
            ((qn_hbm, qn), (wuk_hbm, wuk), (qr_hbm, qr), (wuv_hbm, wuv))
        )
    ]
    for load in loads:
        load.start()

    barrier = pltpu.get_barrier_semaphore()
    for other in (partner, near, far, wide):
        pl.semaphore_signal(barrier, inc=1, device_id={"ctx": other}, device_id_type=MESH)

    for c in range(4):
        held[4, c] = ckv_ref[:blk, c * LANES:(c + 1) * LANES]
        held[4, 5 + c] = ckv_ref[blk:, c * LANES:(c + 1) * LANES]
    held[4, 4, :, :rope] = krope_ref[:blk, :]
    held[4, 4, :, rope:] = krope_ref[blk:, :]
    pl.semaphore_wait(barrier, 4)

    def send(slot_from, slot_to, piece, target):
        start, size = PIECES[piece]
        return pltpu.make_async_remote_copy(
            src_ref=held.at[slot_from, pl.ds(start, size)],
            dst_ref=held.at[slot_to, pl.ds(start, size)],
            send_sem=send_sem.at[slot_to, piece],
            recv_sem=recv_sem.at[slot_to, piece],
            device_id={"ctx": target},
            device_id_type=MESH,
        )

    copies = {}
    for piece in (0, 1):
        for slot, target in ((NEAR, near), (FAR, wide), (PARTNER, partner)):
            copies[slot, piece] = send(4, slot, piece, target)
            copies[slot, piece].start()
        copies[WIDE, piece] = send(NEAR, WIDE, piece, partner)

    loads[0].wait()
    flat[...] = qn[...].astype(jnp.float32).reshape(flat.shape)
    loads[1].wait()
    loads[2].wait()
    flat_rope[...] = qr[...].astype(jnp.float32).reshape(flat_rope.shape)

    for h in range(heads):
        for b in range(2):
            rows = pl.ds(b * blk * heads + h, blk, stride=heads)
            part = flat[rows, :].astype(jnp.bfloat16)
            into = pl.ds(h * blk, blk)
            qs[b, into, :lat] = jnp.dot(
                part, wuk[h], preferred_element_type=jnp.float32
            ).astype(jnp.bfloat16)
            turned = flat_rope[rows, :].astype(jnp.bfloat16)
            qs[b, into, lat:lat + rope] = turned
            qs[b, into, lat + rope:] = turned

    my_pos = pos_ref[2 * me]
    lane = lax.broadcasted_iota(jnp.int32, (blk, LANES), 1)
    chunk = qs.shape[1] // 2

    def gather(slot, low_at, high_at):
        for base, first in ((low_at, 0), (high_at, 5)):
            for c in range(4):
                keys[pl.ds(base, blk), c * LANES:(c + 1) * LANES] = held[slot, first + c]
        both = held[slot, 4]
        zero = jnp.zeros_like(both)
        keys[pl.ds(low_at, blk), lat:] = jnp.where(lane < rope, both, zero)
        keys[pl.ds(high_at, blk), lat:] = jnp.where(lane < rope, zero, both)

    def fold(b, rows, width, hide, first):
        score = nt_dot(qs[b, rows, :], keys[:width, :]) * factor
        score = hide(score)
        best = jnp.max(score, axis=1, keepdims=True)
        if not first:
            old = top_s[b, rows, :1]
            best = jnp.maximum(best, old)
        expo = jnp.exp2(score - best)
        total = jnp.sum(expo, axis=1, keepdims=True)
        part = jnp.dot(
            expo.astype(jnp.bfloat16), keys[:width, :lat], preferred_element_type=jnp.float32
        )
        if not first:
            shrink = jnp.exp2(old - best)
            total = total + sum_s[b, rows, :1] * shrink
            part = part + acc[b, rows, :] * shrink
        acc[b, rows, :] = part
        top_s[b, rows, :] = jnp.broadcast_to(best, (chunk, LANES))
        sum_s[b, rows, :] = jnp.broadcast_to(total, (chunk, LANES))

    def stage(slots, sources, first):
        count = len(slots)
        for i, slot in enumerate(slots):
            gather(slot, i * blk, (count + i) * blk)
        at_key = lax.broadcasted_iota(jnp.int32, (1, count * blk), 1) // blk
        low_bias = jnp.zeros((1, count * blk), jnp.float32)
        high_bias = jnp.zeros((1, count * blk), jnp.float32)
        for i, source in enumerate(sources):
            if source is None:
                continue
            theirs = pos_ref[2 * source]
            low = jnp.where(theirs <= my_pos, 0.0, -1e30)
            high = jnp.where(theirs >= my_pos, 0.0, -1e30)
            low_bias = jnp.where(at_key == i, low, low_bias)
            high_bias = jnp.where(at_key == i, high, high_bias)

        def hide_low(score):
            if not first:
                return score + low_bias
            token = lax.rem(lax.broadcasted_iota(jnp.int32, score.shape, 0), blk)
            key = lax.broadcasted_iota(jnp.int32, score.shape, 1)
            return jnp.where((key <= token) | (key >= blk), score + low_bias, -1e30)

        def hide_high(score):
            half = count * blk
            if not first:
                return jnp.concatenate([score[:, :half], score[:, half:] + high_bias], axis=1)
            token = lax.rem(lax.broadcasted_iota(jnp.int32, (score.shape[0], half), 0), blk)
            key = lax.broadcasted_iota(jnp.int32, (score.shape[0], half), 1)
            right = jnp.where(
                (key <= token) | (key >= blk), score[:, half:] + high_bias, -1e30
            )
            return jnp.concatenate([score[:, :half], right], axis=1)

        def body(c, carry):
            rows = pl.ds(pl.multiple_of(c * chunk, chunk), chunk)
            fold(1, rows, 2 * count * blk, hide_high, first)
            fold(0, rows, count * blk, hide_low, first)
            return carry

        lax.fori_loop(0, 2, body, 0)

    copies[PARTNER, 0].wait_recv()
    copies[PARTNER, 1].wait_recv()
    stage((4, PARTNER), (None, partner), True)

    for piece in (0, 1):
        copies[NEAR, piece].wait_recv()
        copies[WIDE, piece].start()
    copies[FAR, 0].wait_recv()
    copies[FAR, 1].wait_recv()
    stage((NEAR, FAR), (near, far), False)
    copies[WIDE, 0].wait_recv()
    copies[WIDE, 1].wait_recv()
    stage((WIDE,), (wide,), False)

    loads[3].wait()
    for h in range(heads):
        for b in range(2):
            rows = pl.ds(h * blk, blk)
            o_lat = (acc[b, rows, :] / sum_s[b, rows, :1]).astype(jnp.bfloat16)
            flat[pl.ds(b * blk * heads + h, blk, stride=heads), :] = jnp.dot(
                o_lat, wuv[h], preferred_element_type=jnp.float32
            )
    out_ref[...] = flat[...].reshape(out_ref.shape).astype(jnp.bfloat16)
    for key in copies:
        copies[key].wait_send()


def per_device(q_nope, q_rope, c_kv, k_rope, block_pos, w_uk, w_uv):
    rows, heads, nope = q_nope.shape
    blk = rows // 2
    lat = c_kv.shape[1]
    rope = k_rope.shape[1]
    factor = math.log2(math.e) / math.sqrt(nope + rope)
    vmem = pl.BlockSpec(memory_space=pltpu.VMEM)
    anywhere = pl.BlockSpec(memory_space=pl.ANY)
    bf16, f32 = jnp.bfloat16, jnp.float32
    return pl.pallas_call(
        functools.partial(attention_kernel, factor),
        out_shape=jax.ShapeDtypeStruct((rows, heads, w_uv.shape[2]), bf16),
        in_specs=[pl.BlockSpec(memory_space=pltpu.SMEM), vmem, vmem] + [anywhere] * 4,
        out_specs=vmem,
        scratch_shapes=[
            pltpu.VMEM(q_nope.shape, bf16),
            pltpu.VMEM(q_rope.shape, bf16),
            pltpu.VMEM(w_uk.shape, bf16),
            pltpu.VMEM(w_uv.shape, bf16),
            pltpu.VMEM((rows * heads, nope), f32),
            pltpu.VMEM((rows * heads, rope), f32),
            pltpu.VMEM((2, blk * heads, lat + 2 * rope), bf16),
            pltpu.VMEM((5, 9, blk, LANES), bf16),
            pltpu.VMEM((4 * blk, lat + 2 * rope), bf16),
            pltpu.VMEM((2, blk * heads, lat), f32),
            pltpu.VMEM((2, blk * heads, LANES), f32),
            pltpu.VMEM((2, blk * heads, LANES), f32),
            pltpu.SemaphoreType.DMA((4,)),
            pltpu.SemaphoreType.DMA((4, 2)),
            pltpu.SemaphoreType.DMA((4, 2)),
        ],
        compiler_params=pltpu.CompilerParams(
            collective_id=0, has_side_effects=True, vmem_limit_bytes=48 * 1024 * 1024
        ),
        cost_estimate=pl.CostEstimate(
            flops=6 * 10**9, bytes_accessed=5 * 10**6, transcendentals=2 * 10**6
        ),
    )(block_pos, c_kv, k_rope, q_nope, q_rope, w_uk, w_uv)


def solution(mesh):
    placed = (
        P("ctx", "head", None),
        P("ctx", "head", None),
        P("ctx", None),
        P("ctx", None),
        P(),
        P("head", None, None),
        P("head", None, None),
    )
    return jax.shard_map(
        per_device, mesh=mesh, in_specs=placed, out_specs=P("ctx", "head", None), check_vma=False
    )
```

```python
import functools
import math

import jax
import jax.numpy as jnp
from jax import lax
from jax.experimental import pallas as pl
from jax.experimental.pallas import tpu as pltpu
from jax.sharding import PartitionSpec as P

MESH = pl.DeviceIdType.MESH
LANES = 128
PIECES = ((0, 5), (5, 4))
PARTNER, NEAR, FAR, WIDE = 0, 1, 2, 3


def attention_kernel(
    factor,
    pos_ref, ckv_ref, krope_ref, qn_hbm, qr_hbm, wuk_hbm, wuv_hbm, out_ref,
    qn, qr, wuk, wuv, flat, qs, held, keys, values, acc, top_s, sum_s, wall,
    load_sem, send_sem, recv_sem,
):
    n = lax.axis_size("ctx")
    me = lax.axis_index("ctx")
    heads = qn.shape[1]
    blk = ckv_ref.shape[0] // 2
    lat = ckv_ref.shape[1]
    rope = krope_ref.shape[0]
    odd = lax.rem(me, 2)

    def at(by):
        return lax.rem(me + by + n, n)

    partner = at(1 - 2 * odd)
    near = at(2 * odd - 1)
    far = at(4 * odd - 2)
    wide = at(2 - 4 * odd)

    loads = [
        pltpu.make_async_copy(a, b, load_sem.at[i])
        for i, (a, b) in enumerate(
            ((qn_hbm, qn), (wuk_hbm, wuk), (qr_hbm, qr), (wuv_hbm, wuv))
        )
    ]
    for load in loads:
        load.start()

    barrier = pltpu.get_barrier_semaphore()
    for other in (partner, near, far, wide):
        pl.semaphore_signal(barrier, inc=1, device_id={"ctx": other}, device_id_type=MESH)

    for c in range(4):
        held[4, c] = ckv_ref[:blk, c * LANES:(c + 1) * LANES]
        held[4, 5 + c] = ckv_ref[blk:, c * LANES:(c + 1) * LANES]
    held[4, 4, :, :rope] = krope_ref[:, :blk].T
    held[4, 4, :, rope:] = krope_ref[:, blk:].T
    pl.semaphore_wait(barrier, 4)

    def send(slot_from, slot_to, piece, target):
        start, size = PIECES[piece]
        return pltpu.make_async_remote_copy(
            src_ref=held.at[slot_from, pl.ds(start, size)],
            dst_ref=held.at[slot_to, pl.ds(start, size)],
            send_sem=send_sem.at[slot_to, piece],
            recv_sem=recv_sem.at[slot_to, piece],
            device_id={"ctx": target},
            device_id_type=MESH,
        )

    copies = {}
    for piece in (0, 1):
        for slot, target in ((NEAR, near), (FAR, wide), (PARTNER, partner)):
            copies[slot, piece] = send(4, slot, piece, target)
            copies[slot, piece].start()
        copies[WIDE, piece] = send(NEAR, WIDE, piece, partner)

    loads[0].wait()
    flat[...] = qn[...].astype(jnp.float32).reshape(flat.shape)
    loads[1].wait()
    loads[2].wait()
    for h in range(heads):
        part = flat[pl.ds(h, 2 * blk, stride=heads), :].astype(jnp.bfloat16)
        turned = jnp.dot(part, wuk[h], preferred_element_type=jnp.float32).astype(jnp.bfloat16).T
        for b in range(2):
            into = pl.ds(h * blk, blk)
            qs[b, :lat, into] = turned[:, b * blk:(b + 1) * blk]
            rotary = qr[h, :, b * blk:(b + 1) * blk]
            qs[b, lat:lat + rope, into] = rotary
            qs[b, lat + rope:, into] = rotary

    my_pos = pos_ref[2 * me]
    lane = lax.broadcasted_iota(jnp.int32, (blk, LANES), 1)
    wall[...] = jnp.where(
        lax.broadcasted_iota(jnp.int32, (blk, blk), 0)
        <= lax.broadcasted_iota(jnp.int32, (blk, blk), 1),
        0.0,
        -1e30,
    )
    chunk = qs.shape[2] // 2

    def gather(slot, low_at, high_at):
        for base, first in ((low_at, 0), (high_at, 5)):
            for c in range(4):
                piece = held[slot, first + c]
                keys[pl.ds(base, blk), c * LANES:(c + 1) * LANES] = piece
                values[c * LANES:(c + 1) * LANES, pl.ds(base, blk)] = piece.T
        both = held[slot, 4]
        zero = jnp.zeros_like(both)
        keys[pl.ds(low_at, blk), lat:] = jnp.where(lane < rope, both, zero)
        keys[pl.ds(high_at, blk), lat:] = jnp.where(lane < rope, zero, both)

    def fold(b, columns, hides, first):
        width = len(hides) * blk
        score = jnp.dot(
            keys[:width, :], qs[b, :, columns], preferred_element_type=jnp.float32
        ) * factor
        parts = []
        for i, hide in enumerate(hides):
            part = score[i * blk:(i + 1) * blk]
            if hide is wall:
                part = part + jnp.concatenate([wall[...]] * (chunk // blk), axis=1)
            elif hide is not None:
                part = part + hide
            parts.append(part)
        best = functools.reduce(jnp.maximum, parts)
        best = jnp.max(best, axis=0, keepdims=True)
        if not first:
            old = top_s[b, :1, columns]
            best = jnp.maximum(best, old)
        parts = [jnp.exp2(part - best) for part in parts]
        total = jnp.sum(functools.reduce(jnp.add, parts), axis=0, keepdims=True)
        weights = jnp.concatenate([part.astype(jnp.bfloat16) for part in parts], axis=0)
        mixed = jnp.dot(values[:, :width], weights, preferred_element_type=jnp.float32)
        if not first:
            shrink = jnp.exp2(old - best)
            total = total + sum_s[b, :1, columns] * shrink
            mixed = mixed + acc[b, :, columns] * shrink
        acc[b, :, columns] = mixed
        top_s[b, :1, columns] = best
        sum_s[b, :1, columns] = total

    def stage(slots, sources, first):
        count = len(slots)
        low, high = [], []
        for i, (slot, source) in enumerate(zip(slots, sources)):
            gather(slot, i * blk, (count + i) * blk)
            if source is None:
                low.append(wall)
                high.append(wall)
            else:
                theirs = pos_ref[2 * source]
                low.append(jnp.where(theirs <= my_pos, 0.0, -1e30))
                high.append(jnp.where(theirs >= my_pos, 0.0, -1e30))

        def body(c, carry):
            columns = pl.ds(pl.multiple_of(c * chunk, chunk), chunk)
            fold(1, columns, [None] * count + high, first)
            fold(0, columns, low, first)
            return carry

        lax.fori_loop(0, 2, body, 0)

    loads[3].wait()
    copies[PARTNER, 0].wait_recv()
    copies[PARTNER, 1].wait_recv()
    stage((4, PARTNER), (None, partner), True)

    for piece in (0, 1):
        copies[NEAR, piece].wait_recv()
        copies[WIDE, piece].start()
    copies[FAR, 0].wait_recv()
    copies[FAR, 1].wait_recv()
    stage((NEAR, FAR), (near, far), False)
    copies[WIDE, 0].wait_recv()
    copies[WIDE, 1].wait_recv()
    stage((WIDE,), (wide,), False)

    for h in range(heads):
        for b in range(2):
            columns = pl.ds(h * blk, blk)
            o_lat = (acc[b, :, columns] / sum_s[b, :1, columns]).astype(jnp.bfloat16)
            flat[pl.ds(b * blk * heads + h, blk, stride=heads), :] = jnp.dot(
                o_lat.T, wuv[h], preferred_element_type=jnp.float32
            )
    out_ref[...] = flat[...].reshape(out_ref.shape).astype(jnp.bfloat16)
    for key in copies:
        copies[key].wait_send()


def per_device(q_nope, q_rope, c_kv, k_rope, block_pos, w_uk, w_uv):
    rows, heads, nope = q_nope.shape
    blk = rows // 2
    lat = c_kv.shape[1]
    rope = k_rope.shape[1]
    factor = math.log2(math.e) / math.sqrt(nope + rope)
    vmem = pl.BlockSpec(memory_space=pltpu.VMEM)
    anywhere = pl.BlockSpec(memory_space=pl.ANY)
    bf16, f32 = jnp.bfloat16, jnp.float32
    return pl.pallas_call(
        functools.partial(attention_kernel, factor),
        out_shape=jax.ShapeDtypeStruct((rows, heads, w_uv.shape[2]), bf16),
        in_specs=[pl.BlockSpec(memory_space=pltpu.SMEM), vmem, vmem] + [anywhere] * 4,
        out_specs=vmem,
        scratch_shapes=[
            pltpu.VMEM(q_nope.shape, bf16),
            pltpu.VMEM((heads, rope, rows), bf16),
            pltpu.VMEM(w_uk.shape, bf16),
            pltpu.VMEM(w_uv.shape, bf16),
            pltpu.VMEM((rows * heads, nope), f32),
            pltpu.VMEM((2, lat + 2 * rope, blk * heads), bf16),
            pltpu.VMEM((5, 9, blk, LANES), bf16),
            pltpu.VMEM((4 * blk, lat + 2 * rope), bf16),
            pltpu.VMEM((lat, 4 * blk), bf16),
            pltpu.VMEM((2, lat, blk * heads), f32),
            pltpu.VMEM((2, 8, blk * heads), f32),
            pltpu.VMEM((2, 8, blk * heads), f32),
            pltpu.VMEM((blk, blk), f32),
            pltpu.SemaphoreType.DMA((4,)),
            pltpu.SemaphoreType.DMA((4, 2)),
            pltpu.SemaphoreType.DMA((4, 2)),
        ],
        compiler_params=pltpu.CompilerParams(
            collective_id=0, has_side_effects=True, vmem_limit_bytes=60 * 1024 * 1024
        ),
        cost_estimate=pl.CostEstimate(
            flops=6 * 10**9, bytes_accessed=5 * 10**6, transcendentals=2 * 10**6
        ),
    )(block_pos, c_kv, k_rope.T, q_nope, jnp.transpose(q_rope, (1, 2, 0)), w_uk, w_uv)


def solution(mesh):
    placed = (
        P("ctx", "head", None),
        P("ctx", "head", None),
        P("ctx", None),
        P("ctx", None),
        P(),
        P("head", None, None),
        P("head", None, None),
    )
    return jax.shard_map(
        per_device, mesh=mesh, in_specs=placed, out_specs=P("ctx", "head", None), check_vma=False
    )
```

```python
import functools
import math

import jax
import jax.numpy as jnp
from jax import lax
from jax.experimental import pallas as pl
from jax.experimental.pallas import tpu as pltpu
from jax.sharding import PartitionSpec as P

MESH = pl.DeviceIdType.MESH
LANES = 128
PIECES = ((0, 5), (5, 4))
PARTNER, NEAR, FAR, WIDE = 0, 1, 2, 3


def attention_kernel(
    factor,
    pos_ref, ckv_hbm, krope_hbm, qn_hbm, qr_hbm, wuk_hbm, wuv_hbm, out_ref,
    ckv_ref, krope_ref, qn, qr, wuk, wuv, flat, qs, held, keys, values, acc, top_s, sum_s, wall,
    load_sem, send_sem, recv_sem,
):
    n = lax.axis_size("ctx")
    me = lax.axis_index("ctx")
    heads = qn.shape[1]
    blk = ckv_ref.shape[0] // 2
    lat = ckv_ref.shape[1]
    rope = krope_ref.shape[0]
    core = lax.rem(me, 2)
    side = lax.rem(lax.div(me, 2), 2)
    inner = lax.rem(core + side, 2)
    toward = 1 - 2 * side

    def at(by):
        return lax.rem(me + by + n, n)

    partner = at(1 - 2 * core)
    near = at(2 * core - 1)
    far = at(4 * core - 2)
    wide = at(2 - 4 * core)
    across = at(2 * toward)
    relay = at(3 * toward * (2 * inner - 1))

    loads = [
        pltpu.make_async_copy(a, b, load_sem.at[i])
        for i, (a, b) in enumerate(
            ((ckv_hbm, ckv_ref), (krope_hbm, krope_ref), (qn_hbm, qn),
             (wuk_hbm, wuk), (qr_hbm, qr), (wuv_hbm, wuv))
        )
    ]
    for load in loads:
        load.start()

    barrier = pltpu.get_barrier_semaphore()
    for other in (partner, near, across, relay):
        pl.semaphore_signal(barrier, inc=1, device_id={"ctx": other}, device_id_type=MESH)

    loads[0].wait()
    loads[1].wait()
    for c in range(4):
        held[4, c] = ckv_ref[:blk, c * LANES:(c + 1) * LANES]
        held[4, 5 + c] = ckv_ref[blk:, c * LANES:(c + 1) * LANES]
    held[4, 4, :, :rope] = krope_ref[:, :blk].T
    held[4, 4, :, rope:] = krope_ref[:, blk:].T
    pl.semaphore_wait(barrier, 4)

    def send(slot_from, slot_to, piece, target, flag=None):
        start, size = PIECES[piece]
        return pltpu.make_async_remote_copy(
            src_ref=held.at[slot_from, pl.ds(start, size)],
            dst_ref=held.at[slot_to, pl.ds(start, size)],
            send_sem=send_sem.at[slot_to if flag is None else flag, piece],
            recv_sem=recv_sem.at[slot_to, piece],
            device_id={"ctx": target},
            device_id_type=MESH,
        )

    def arrived(slot, piece):
        send(slot, slot, piece, partner).wait_recv()

    own = []
    for piece in (0, 1):
        own.append(send(4, 2 - inner, piece, at(toward * (2 - inner))))
        own.append(send(4, PARTNER, piece, partner))
    for copy in own:
        copy.start()
    forward = [send(NEAR, WIDE, piece, partner) for piece in (0, 1)]
    relays = [
        send(a, b, piece, relay, flag)
        for piece in (0, 1)
        for a, b, flag in ((FAR, NEAR, 4), (NEAR, FAR, FAR))
    ]

    def pass_on(piece):
        arrived(FAR, piece)
        relays[2 * piece].start()
        arrived(NEAR, piece)
        relays[2 * piece + 1].start()
        forward[piece].start()

    loads[2].wait()
    flat[...] = qn[...].astype(jnp.float32).reshape(flat.shape)
    loads[3].wait()
    loads[4].wait()
    for h in range(heads):
        part = flat[pl.ds(h, 2 * blk, stride=heads), :].astype(jnp.bfloat16)
        turned = jnp.dot(part, wuk[h], preferred_element_type=jnp.float32).astype(jnp.bfloat16).T
        for b in range(2):
            into = pl.ds(h * blk, blk)
            qs[b, :lat, into] = turned[:, b * blk:(b + 1) * blk]
            rotary = qr[h, :, b * blk:(b + 1) * blk]
            qs[b, lat:lat + rope, into] = rotary
            qs[b, lat + rope:, into] = rotary

    my_pos = pos_ref[2 * me]
    lane = lax.broadcasted_iota(jnp.int32, (blk, LANES), 1)
    wall[...] = jnp.where(
        lax.broadcasted_iota(jnp.int32, (blk, blk), 0)
        <= lax.broadcasted_iota(jnp.int32, (blk, blk), 1),
        0.0,
        -1e30,
    )
    chunk = qs.shape[2] // 2

    def gather(slot, low_at, high_at):
        for base, first in ((low_at, 0), (high_at, 5)):
            for c in range(4):
                piece = held[slot, first + c]
                keys[pl.ds(base, blk), c * LANES:(c + 1) * LANES] = piece
                values[c * LANES:(c + 1) * LANES, pl.ds(base, blk)] = piece.T
        both = held[slot, 4]
        zero = jnp.zeros_like(both)
        keys[pl.ds(low_at, blk), lat:] = jnp.where(lane < rope, both, zero)
        keys[pl.ds(high_at, blk), lat:] = jnp.where(lane < rope, zero, both)

    def fold(b, columns, hides, first):
        width = len(hides) * blk
        score = jnp.dot(
            keys[:width, :], qs[b, :, columns], preferred_element_type=jnp.float32
        ) * factor
        parts = []
        for i, hide in enumerate(hides):
            part = score[i * blk:(i + 1) * blk]
            if hide is wall:
                part = part + jnp.concatenate([wall[...]] * (chunk // blk), axis=1)
            elif hide is not None:
                part = part + hide
            parts.append(part)
        best = functools.reduce(jnp.maximum, parts)
        best = jnp.max(best, axis=0, keepdims=True)
        if not first:
            old = top_s[b, :1, columns]
            best = jnp.maximum(best, old)
        parts = [jnp.exp2(part - best) for part in parts]
        total = jnp.sum(functools.reduce(jnp.add, parts), axis=0, keepdims=True)
        weights = jnp.concatenate([part.astype(jnp.bfloat16) for part in parts], axis=0)
        mixed = jnp.dot(values[:, :width], weights, preferred_element_type=jnp.float32)
        if not first:
            shrink = jnp.exp2(old - best)
            total = total + sum_s[b, :1, columns] * shrink
            mixed = mixed + acc[b, :, columns] * shrink
        acc[b, :, columns] = mixed
        top_s[b, :1, columns] = best
        sum_s[b, :1, columns] = total

    def stage(slots, sources, first, between=None):
        count = len(slots)
        low, high = [], []
        for i, (slot, source) in enumerate(zip(slots, sources)):
            gather(slot, i * blk, (count + i) * blk)
            if source is None:
                low.append(wall)
                high.append(wall)
            else:
                theirs = pos_ref[2 * source]
                low.append(jnp.where(theirs <= my_pos, 0.0, -1e30))
                high.append(jnp.where(theirs >= my_pos, 0.0, -1e30))

        def body(c, carry):
            columns = pl.ds(c * chunk if isinstance(c, int) else pl.multiple_of(c * chunk, chunk), chunk)
            fold(1, columns, [None] * count + high, first)
            fold(0, columns, low, first)
            return carry

        if between is None:
            lax.fori_loop(0, 2, body, 0)
        else:
            body(0, 0)
            between()
            body(1, 0)

    def pass_low():
        @pl.when(inner == 1)
        def _():
            pass_on(0)

    loads[5].wait()
    arrived(PARTNER, 0)
    arrived(PARTNER, 1)
    stage((4, PARTNER), (None, partner), True, pass_low)

    @pl.when(inner == 1)
    def _():
        pass_on(1)
        stage((NEAR, FAR), (near, far), False)

    arrived(WIDE, 0)
    arrived(WIDE, 1)
    stage((WIDE,), (wide,), False)

    @pl.when(inner == 0)
    def _():
        for piece in (0, 1):
            arrived(NEAR, piece)
            forward[piece].start()
        arrived(FAR, 0)
        arrived(FAR, 1)
        stage((NEAR, FAR), (near, far), False)

    for h in range(heads):
        for b in range(2):
            columns = pl.ds(h * blk, blk)
            o_lat = (acc[b, :, columns] / sum_s[b, :1, columns]).astype(jnp.bfloat16)
            flat[pl.ds(b * blk * heads + h, blk, stride=heads), :] = jnp.dot(
                o_lat.T, wuv[h], preferred_element_type=jnp.float32
            )
    out_ref[...] = flat[...].reshape(out_ref.shape).astype(jnp.bfloat16)
    for copy in own + forward:
        copy.wait_send()

    @pl.when(inner == 1)
    def _():
        for copy in relays:
            copy.wait_send()


def per_device(q_nope, q_rope, c_kv, k_rope, block_pos, w_uk, w_uv):
    rows, heads, nope = q_nope.shape
    blk = rows // 2
    lat = c_kv.shape[1]
    rope = k_rope.shape[1]
    factor = math.log2(math.e) / math.sqrt(nope + rope)
    vmem = pl.BlockSpec(memory_space=pltpu.VMEM)
    anywhere = pl.BlockSpec(memory_space=pltpu.HBM)
    bf16, f32 = jnp.bfloat16, jnp.float32
    return pl.pallas_call(
        functools.partial(attention_kernel, factor),
        out_shape=jax.ShapeDtypeStruct((rows, heads, w_uv.shape[2]), bf16),
        in_specs=[pl.BlockSpec(memory_space=pltpu.SMEM)] + [anywhere] * 6,
        out_specs=vmem,
        scratch_shapes=[
            pltpu.VMEM(c_kv.shape, bf16),
            pltpu.VMEM((rope, rows), bf16),
            pltpu.VMEM(q_nope.shape, bf16),
            pltpu.VMEM((heads, rope, rows), bf16),
            pltpu.VMEM(w_uk.shape, bf16),
            pltpu.VMEM(w_uv.shape, bf16),
            pltpu.VMEM((rows * heads, nope), f32),
            pltpu.VMEM((2, lat + 2 * rope, blk * heads), bf16),
            pltpu.VMEM((5, 9, blk, LANES), bf16),
            pltpu.VMEM((4 * blk, lat + 2 * rope), bf16),
            pltpu.VMEM((lat, 4 * blk), bf16),
            pltpu.VMEM((2, lat, blk * heads), f32),
            pltpu.VMEM((2, 8, blk * heads), f32),
            pltpu.VMEM((2, 8, blk * heads), f32),
            pltpu.VMEM((blk, blk), f32),
            pltpu.SemaphoreType.DMA((6,)),
            pltpu.SemaphoreType.DMA((5, 2)),
            pltpu.SemaphoreType.DMA((4, 2)),
        ],
        compiler_params=pltpu.CompilerParams(
            collective_id=0, has_side_effects=True, vmem_limit_bytes=40 * 1024 * 1024
        ),
        cost_estimate=pl.CostEstimate(
            flops=6 * 10**9, bytes_accessed=5 * 10**6, transcendentals=2 * 10**6
        ),
    )(block_pos, c_kv, k_rope.T, q_nope, jnp.transpose(q_rope, (1, 2, 0)), w_uk, w_uv)


def solution(mesh):
    placed = (
        P("ctx", "head", None),
        P("ctx", "head", None),
        P("ctx", None),
        P("ctx", None),
        P(),
        P("head", None, None),
        P("head", None, None),
    )
    return jax.shard_map(
        per_device, mesh=mesh, in_specs=placed, out_specs=P("ctx", "head", None), check_vma=False
    )
```

```python
import functools
import math

import jax
import jax.numpy as jnp
from jax import lax
from jax.experimental import pallas as pl
from jax.experimental.pallas import tpu as pltpu
from jax.sharding import PartitionSpec as P

MESH = pl.DeviceIdType.MESH
LANES = 128
PIECES = ((0, 3), (3, 2), (5, 2), (7, 2))
PARTNER, NEAR, FAR, WIDE = 0, 1, 2, 3


def attention_kernel(
    factor,
    pos_ref, ckv_hbm, krope_hbm, qn_hbm, qr_hbm, wuk_hbm, wuv_hbm, out_ref,
    ckv_ref, krope_ref, qn, qr, wuk, wuv, flat, qs, held, keys, values, acc, top_s, sum_s, wall,
    load_sem, send_sem, recv_sem,
):
    n = lax.axis_size("ctx")
    me = lax.axis_index("ctx")
    heads = qn.shape[1]
    blk = ckv_ref.shape[0] // 2
    lat = ckv_ref.shape[1]
    rope = krope_ref.shape[0]
    core = lax.rem(me, 2)
    side = lax.rem(lax.div(me, 2), 2)
    inner = lax.rem(core + side, 2)
    toward = 1 - 2 * side

    def at(by):
        return lax.rem(me + by + n, n)

    partner = at(1 - 2 * core)
    near = at(2 * core - 1)
    far = at(4 * core - 2)
    wide = at(2 - 4 * core)
    across = at(2 * toward)
    relay = at(3 * toward * (2 * inner - 1))

    loads = [
        pltpu.make_async_copy(a, b, load_sem.at[i])
        for i, (a, b) in enumerate(
            ((ckv_hbm, ckv_ref), (krope_hbm, krope_ref), (qn_hbm, qn),
             (wuk_hbm, wuk), (qr_hbm, qr), (wuv_hbm, wuv))
        )
    ]
    for load in loads:
        load.start()

    barrier = pltpu.get_barrier_semaphore()
    for other in (partner, near, across, relay):
        pl.semaphore_signal(barrier, inc=1, device_id={"ctx": other}, device_id_type=MESH)

    loads[0].wait()
    loads[1].wait()
    for c in range(4):
        held[4, c] = ckv_ref[:blk, c * LANES:(c + 1) * LANES]
        held[4, 5 + c] = ckv_ref[blk:, c * LANES:(c + 1) * LANES]
    held[4, 4, :, :rope] = krope_ref[:, :blk].T
    held[4, 4, :, rope:] = krope_ref[:, blk:].T
    pl.semaphore_wait(barrier, 4)

    def send(slot_from, slot_to, piece, target, flag=None):
        start, size = PIECES[piece]
        return pltpu.make_async_remote_copy(
            src_ref=held.at[slot_from, pl.ds(start, size)],
            dst_ref=held.at[slot_to, pl.ds(start, size)],
            send_sem=send_sem.at[slot_to if flag is None else flag, piece],
            recv_sem=recv_sem.at[slot_to, piece],
            device_id={"ctx": target},
            device_id_type=MESH,
        )

    def arrived(slot, piece):
        send(slot, slot, piece, partner).wait_recv()

    own = []
    for piece in range(len(PIECES)):
        own.append(send(4, 2 - inner, piece, at(toward * (2 - inner))))
        own.append(send(4, PARTNER, piece, partner))
    for copy in own:
        copy.start()
    forward = [send(NEAR, WIDE, piece, partner) for piece in range(len(PIECES))]
    relays = [
        send(a, b, piece, relay, flag)
        for piece in range(len(PIECES))
        for a, b, flag in ((FAR, NEAR, 4), (NEAR, FAR, FAR))
    ]

    def pass_on(piece):
        arrived(FAR, piece)
        relays[2 * piece].start()
        arrived(NEAR, piece)
        relays[2 * piece + 1].start()
        forward[piece].start()

    loads[2].wait()
    flat[...] = qn[...].astype(jnp.float32).reshape(flat.shape)
    loads[3].wait()
    loads[4].wait()
    for h in range(heads):
        part = flat[pl.ds(h, 2 * blk, stride=heads), :].astype(jnp.bfloat16)
        turned = jnp.dot(part, wuk[h], preferred_element_type=jnp.float32).astype(jnp.bfloat16).T
        for b in range(2):
            into = pl.ds(h * blk, blk)
            qs[b, :lat, into] = turned[:, b * blk:(b + 1) * blk]
            rotary = qr[h, :, b * blk:(b + 1) * blk]
            qs[b, lat:lat + rope, into] = rotary
            qs[b, lat + rope:, into] = rotary

    my_pos = pos_ref[2 * me]
    lane = lax.broadcasted_iota(jnp.int32, (blk, LANES), 1)
    wall[...] = jnp.where(
        lax.broadcasted_iota(jnp.int32, (blk, blk), 0)
        <= lax.broadcasted_iota(jnp.int32, (blk, blk), 1),
        0.0,
        -1e30,
    )
    chunk = qs.shape[2] // 2

    def gather_low(slot, base):
        for c in range(4):
            piece = held[slot, c]
            keys[pl.ds(base, blk), c * LANES:(c + 1) * LANES] = piece
            values[c * LANES:(c + 1) * LANES, pl.ds(base, blk)] = piece.T
        both = held[slot, 4]
        keys[pl.ds(base, blk), lat:] = jnp.where(lane < rope, both, jnp.zeros_like(both))

    def gather_high(slot, base):
        for c in range(4):
            piece = held[slot, 5 + c]
            keys[pl.ds(base, blk), c * LANES:(c + 1) * LANES] = piece
            values[c * LANES:(c + 1) * LANES, pl.ds(base, blk)] = piece.T
        both = held[slot, 4]
        keys[pl.ds(base, blk), lat:] = jnp.where(lane < rope, jnp.zeros_like(both), both)

    def fold(b, columns, base, hides, first=False):
        rows = pl.ds(base, len(hides) * blk)
        score = jnp.dot(
            keys[rows, :], qs[b, :, columns], preferred_element_type=jnp.float32
        ) * factor
        parts = []
        for i, hide in enumerate(hides):
            part = score[i * blk:(i + 1) * blk]
            if hide is wall:
                part = part + jnp.concatenate([wall[...]] * (chunk // blk), axis=1)
            elif hide is not None:
                part = part + hide
            parts.append(part)
        best = functools.reduce(jnp.maximum, parts)
        best = jnp.max(best, axis=0, keepdims=True)
        if not first:
            old = top_s[b, :1, columns]
            best = jnp.maximum(best, old)
        parts = [jnp.exp2(part - best) for part in parts]
        total = jnp.sum(functools.reduce(jnp.add, parts), axis=0, keepdims=True)
        weights = jnp.concatenate([part.astype(jnp.bfloat16) for part in parts], axis=0)
        mixed = jnp.dot(values[:, rows], weights, preferred_element_type=jnp.float32)
        if not first:
            shrink = jnp.exp2(old - best)
            total = total + sum_s[b, :1, columns] * shrink
            mixed = mixed + acc[b, :, columns] * shrink
        acc[b, :, columns] = mixed
        top_s[b, :1, columns] = best
        sum_s[b, :1, columns] = total

    def part_of(c):
        return pl.ds(c * chunk if isinstance(c, int) else pl.multiple_of(c * chunk, chunk), chunk)

    def both_chunks(body):
        def step(c, carry):
            body(part_of(c))
            return carry

        lax.fori_loop(0, 2, step, 0)

    def low_hide(source):
        return jnp.where(pos_ref[2 * source] <= my_pos, 0.0, -1e30)

    def high_hide(source):
        return jnp.where(pos_ref[2 * source] >= my_pos, 0.0, -1e30)

    def inner_passes(piece):
        @pl.when(inner == 1)
        def _():
            pass_on(piece)

    def outer_passes(piece):
        @pl.when(inner == 0)
        def _():
            arrived(NEAR, piece)
            forward[piece].start()

    loads[5].wait()
    inner_passes(0)
    for piece in range(len(PIECES)):
        arrived(PARTNER, piece)
    gather_low(4, 0)
    gather_low(PARTNER, blk)
    gather_high(4, 2 * blk)
    gather_high(PARTNER, 3 * blk)
    lows, highs = [wall, low_hide(partner)], [wall, high_hide(partner)]
    fold(1, part_of(0), 0, [None, None] + highs, True)
    fold(0, part_of(0), 0, lows, True)
    inner_passes(1)
    fold(1, part_of(1), 0, [None, None] + highs, True)
    inner_passes(2)
    fold(0, part_of(1), 0, lows, True)
    inner_passes(3)

    near_lows, near_highs = [low_hide(near), low_hide(far)], [high_hide(near), high_hide(far)]

    @pl.when(inner == 1)
    def _():
        gather_low(NEAR, 0)
        gather_low(FAR, blk)
        gather_high(NEAR, 2 * blk)
        gather_high(FAR, 3 * blk)

        @both_chunks
        def _(columns):
            fold(1, columns, 0, [None, None] + near_highs)
            fold(0, columns, 0, near_lows)

    outer_passes(0)
    arrived(WIDE, 0)
    arrived(WIDE, 1)
    gather_low(WIDE, 0)

    @both_chunks
    def _(columns):
        fold(1, columns, 0, [None])
        fold(0, columns, 0, [low_hide(wide)])

    outer_passes(1)
    arrived(WIDE, 2)
    arrived(WIDE, 3)
    gather_high(WIDE, blk)

    @both_chunks
    def _(columns):
        fold(1, columns, blk, [high_hide(wide)])

    @pl.when(inner == 0)
    def _():
        arrived(FAR, 0)
        arrived(FAR, 1)
        gather_low(NEAR, 0)
        gather_low(FAR, blk)

        @both_chunks
        def _(columns):
            fold(1, columns, 0, [None, None])
            fold(0, columns, 0, near_lows)

    outer_passes(2)
    outer_passes(3)

    @pl.when(inner == 0)
    def _():
        arrived(FAR, 2)
        arrived(FAR, 3)
        gather_high(NEAR, 2 * blk)
        gather_high(FAR, 3 * blk)

        @both_chunks
        def _(columns):
            fold(1, columns, 2 * blk, near_highs)

    for h in range(heads):
        for b in range(2):
            columns = pl.ds(h * blk, blk)
            o_lat = (acc[b, :, columns] * (1.0 / sum_s[b, :1, columns])).astype(jnp.bfloat16)
            flat[pl.ds(b * blk * heads + h, blk, stride=heads), :] = jnp.dot(
                o_lat.T, wuv[h], preferred_element_type=jnp.float32
            )
    out_ref[...] = flat[...].reshape(out_ref.shape).astype(jnp.bfloat16)
    for copy in own + forward:
        copy.wait_send()

    @pl.when(inner == 1)
    def _():
        for copy in relays:
            copy.wait_send()


def per_device(q_nope, q_rope, c_kv, k_rope, block_pos, w_uk, w_uv):
    rows, heads, nope = q_nope.shape
    blk = rows // 2
    lat = c_kv.shape[1]
    rope = k_rope.shape[1]
    factor = math.log2(math.e) / math.sqrt(nope + rope)
    vmem = pl.BlockSpec(memory_space=pltpu.VMEM)
    anywhere = pl.BlockSpec(memory_space=pltpu.HBM)
    bf16, f32 = jnp.bfloat16, jnp.float32
    return pl.pallas_call(
        functools.partial(attention_kernel, factor),
        out_shape=jax.ShapeDtypeStruct((rows, heads, w_uv.shape[2]), bf16),
        in_specs=[pl.BlockSpec(memory_space=pltpu.SMEM)] + [anywhere] * 6,
        out_specs=vmem,
        scratch_shapes=[
            pltpu.VMEM(c_kv.shape, bf16),
            pltpu.VMEM((rope, rows), bf16),
            pltpu.VMEM(q_nope.shape, bf16),
            pltpu.VMEM((heads, rope, rows), bf16),
            pltpu.VMEM(w_uk.shape, bf16),
            pltpu.VMEM(w_uv.shape, bf16),
            pltpu.VMEM((rows * heads, nope), f32),
            pltpu.VMEM((2, lat + 2 * rope, blk * heads), bf16),
            pltpu.VMEM((5, 9, blk, LANES), bf16),
            pltpu.VMEM((4 * blk, lat + 2 * rope), bf16),
            pltpu.VMEM((lat, 4 * blk), bf16),
            pltpu.VMEM((2, lat, blk * heads), f32),
            pltpu.VMEM((2, 8, blk * heads), f32),
            pltpu.VMEM((2, 8, blk * heads), f32),
            pltpu.VMEM((blk, blk), f32),
            pltpu.SemaphoreType.DMA((6,)),
            pltpu.SemaphoreType.DMA((5, len(PIECES))),
            pltpu.SemaphoreType.DMA((4, len(PIECES))),
        ],
        compiler_params=pltpu.CompilerParams(
            collective_id=0, has_side_effects=True, vmem_limit_bytes=60 * 1024 * 1024
        ),
        cost_estimate=pl.CostEstimate(
            flops=6 * 10**9, bytes_accessed=5 * 10**6, transcendentals=2 * 10**6
        ),
    )(block_pos, c_kv, k_rope.T, q_nope, jnp.transpose(q_rope, (1, 2, 0)), w_uk, w_uv)


def solution(mesh):
    placed = (
        P("ctx", "head", None),
        P("ctx", "head", None),
        P("ctx", None),
        P("ctx", None),
        P(),
        P("head", None, None),
        P("head", None, None),
    )
    return jax.shard_map(
        per_device, mesh=mesh, in_specs=placed, out_specs=P("ctx", "head", None), check_vma=False
    )
```

```python
import functools
import math

import jax
import jax.numpy as jnp
from jax import lax
from jax.experimental import pallas as pl
from jax.experimental.pallas import tpu as pltpu
from jax.sharding import PartitionSpec as P

MESH = pl.DeviceIdType.MESH
LANES = 128
PARTNER, NEAR, FAR, WIDE = 0, 1, 2, 3


def attention_kernel(
    factor,
    pos_ref, ckv_hbm, krope_hbm, qn_hbm, qr_hbm, wuk_hbm, wuv_hbm, out_ref,
    ckv_ref, krope_ref, qn, qr, wuk, wuv, flat, qs, held, keys, values, acc, top_s, sum_s, wall,
    load_sem, send_sem, recv_sem,
):
    n = lax.axis_size("ctx")
    me = lax.axis_index("ctx")
    heads = qn.shape[1]
    blk = ckv_ref.shape[0] // 2
    lat = ckv_ref.shape[1]
    rope = krope_ref.shape[0]
    mine = lax.axis_index("head")
    core = lax.rem(me, 2)
    side = lax.rem(lax.div(me, 2), 2)
    inner = lax.rem(core + side, 2)
    toward = 1 - 2 * side

    def at(by):
        return lax.rem(me + by + n, n)

    partner = at(1 - 2 * core)
    near = at(2 * core - 1)
    far = at(4 * core - 2)
    wide = at(2 - 4 * core)
    across = at(2 * toward)
    relay = at(3 * toward * (2 * inner - 1))

    loads = [
        pltpu.make_async_copy(a, b, load_sem.at[i])
        for i, (a, b) in enumerate(
            ((ckv_hbm, ckv_ref), (krope_hbm, krope_ref), (qn_hbm, qn),
             (wuk_hbm, wuk), (qr_hbm, qr), (wuv_hbm, wuv))
        )
    ]
    for load in loads:
        load.start()

    barrier = pltpu.get_barrier_semaphore()
    for other in (partner, near, across, relay):
        pl.semaphore_signal(barrier, inc=1, device_id={"ctx": other}, device_id_type=MESH)
    pl.semaphore_signal(barrier, inc=1, device_id={"head": 1 - mine}, device_id_type=MESH)

    loads[0].wait()
    loads[1].wait()
    half = blk // 2
    for b in range(2):
        for c in range(4):
            for r in range(2):
                held[4, b, 2 * c + r] = ckv_ref[
                    pl.ds(b * blk + r * half, half), c * LANES:(c + 1) * LANES
                ]
        turned = krope_ref[:, b * blk:(b + 1) * blk].T
        held[4, b, 8, :, :rope] = turned[:half]
        held[4, b, 8, :, rope:] = turned[half:]
    pl.semaphore_wait(barrier, 5)

    def send(slot_from, slot_to, part, target, flag):
        return pltpu.make_async_remote_copy(
            src_ref=held.at[slot_from, part],
            dst_ref=held.at[slot_to, part],
            send_sem=send_sem.at[flag],
            recv_sem=recv_sem.at[slot_to, part],
            device_id=target,
            device_id_type=MESH,
        )

    def arrived(slot, part):
        send(slot, slot, part, {"ctx": partner}, 0).wait_recv()

    own = [
        send(4, 2 - inner, mine, {"ctx": at(toward * (2 - inner))}, 0),
        send(4, PARTNER, 0, {"ctx": partner}, 1),
        send(4, PARTNER, 1, {"ctx": partner}, 2),
    ]
    for copy in own:
        copy.start()
    relays = [send(NEAR, FAR, mine, {"ctx": relay}, 3), send(FAR, NEAR, mine, {"ctx": relay}, 4)]
    mirrored = [send(slot, slot, mine, {"head": 1 - mine}, 4 + slot) for slot in (NEAR, FAR)]
    forward = [
        send(NEAR, WIDE, mine, {"ctx": partner}, 7),
        send(NEAR, WIDE, 1 - mine, {"ctx": partner}, 8),
    ]

    def pass_mine(relayed):
        for i, slot in enumerate((NEAR, FAR)):
            arrived(slot, mine)
            if relayed:
                relays[i].start()
            mirrored[i].start()
        forward[0].start()

    def pass_theirs():
        arrived(NEAR, 1 - mine)
        forward[1].start()
        arrived(FAR, 1 - mine)

    loads[2].wait()
    flat[...] = qn[...].astype(jnp.float32).reshape(flat.shape)
    loads[3].wait()
    loads[4].wait()
    for h in range(heads):
        part = flat[pl.ds(h, 2 * blk, stride=heads), :].astype(jnp.bfloat16)
        turned = jnp.dot(part, wuk[h], preferred_element_type=jnp.float32).astype(jnp.bfloat16).T
        for b in range(2):
            into = pl.ds(h * blk, blk)
            qs[b, :lat, into] = turned[:, b * blk:(b + 1) * blk]
            rotary = qr[h, :, b * blk:(b + 1) * blk]
            qs[b, lat:lat + rope, into] = rotary
            qs[b, lat + rope:, into] = rotary

    my_pos = pos_ref[2 * me]
    lane = lax.broadcasted_iota(jnp.int32, (half, LANES), 1)
    wall[...] = jnp.where(
        lax.broadcasted_iota(jnp.int32, (blk, blk), 0)
        <= lax.broadcasted_iota(jnp.int32, (blk, blk), 1),
        0.0,
        -1e30,
    )
    chunk = qs.shape[2] // 2

    def gather(slot, part, base):
        for c in range(4):
            tile = held[slot, part, 2 * c:2 * c + 2].reshape(blk, LANES)
            keys[pl.ds(base, blk), c * LANES:(c + 1) * LANES] = tile
            values[c * LANES:(c + 1) * LANES, pl.ds(base, blk)] = tile.T
        both = held[slot, part, 8]
        zero = jnp.zeros_like(both)
        keys[pl.ds(base, half), lat:] = jnp.where(lane < rope, both, zero)
        keys[pl.ds(base + half, half), lat:] = jnp.where(lane < rope, zero, both)

    def fold(b, columns, base, hides, first=False):
        rows = pl.ds(base, len(hides) * blk)
        score = jnp.dot(
            keys[rows, :], qs[b, :, columns], preferred_element_type=jnp.float32
        ) * factor
        parts = []
        for i, hide in enumerate(hides):
            part = score[i * blk:(i + 1) * blk]
            if hide is wall:
                part = part + jnp.concatenate([wall[...]] * (chunk // blk), axis=1)
            elif hide is not None:
                part = part + hide
            parts.append(part)
        best = functools.reduce(jnp.maximum, parts)
        best = jnp.max(best, axis=0, keepdims=True)
        if not first:
            old = top_s[b, :1, columns]
            best = jnp.maximum(best, old)
        parts = [jnp.exp2(part - best) for part in parts]
        total = jnp.sum(functools.reduce(jnp.add, parts), axis=0, keepdims=True)
        weights = jnp.concatenate([part.astype(jnp.bfloat16) for part in parts], axis=0)
        mixed = jnp.dot(values[:, rows], weights, preferred_element_type=jnp.float32)
        if not first:
            shrink = jnp.exp2(old - best)
            total = total + sum_s[b, :1, columns] * shrink
            mixed = mixed + acc[b, :, columns] * shrink
        acc[b, :, columns] = mixed
        top_s[b, :1, columns] = best
        sum_s[b, :1, columns] = total

    def part_of(c):
        return pl.ds(c * chunk if isinstance(c, int) else pl.multiple_of(c * chunk, chunk), chunk)

    def both_chunks(body):
        def step(c, carry):
            body(part_of(c))
            return carry

        lax.fori_loop(0, 2, step, 0)

    def low_hide(source):
        return jnp.where(pos_ref[2 * source] <= my_pos, 0.0, -1e30)

    def high_hide(source):
        return jnp.where(pos_ref[2 * source] >= my_pos, 0.0, -1e30)

    def when(cond):
        return lambda body: pl.when(cond)(body)

    loads[5].wait()
    arrived(PARTNER, 0)
    arrived(PARTNER, 1)
    for i, slot in enumerate((4, PARTNER)):
        gather(slot, 0, i * blk)
        gather(slot, 1, (2 + i) * blk)
    lows, highs = [wall, low_hide(partner)], [wall, high_hide(partner)]
    fold(1, part_of(0), 0, [None, None] + highs, True)

    @when(inner == 1)
    def _():
        pass_mine(True)

    fold(0, part_of(0), 0, lows, True)
    fold(1, part_of(1), 0, [None, None] + highs, True)
    fold(0, part_of(1), 0, lows, True)
    near_lows, near_highs = [low_hide(near), low_hide(far)], [high_hide(near), high_hide(far)]

    def low_unit():
        gather(NEAR, 0, 0)
        gather(FAR, 0, blk)

        @both_chunks
        def _(columns):
            fold(1, columns, 0, [None, None])
            fold(0, columns, 0, near_lows)

    def high_unit():
        gather(NEAR, 1, 2 * blk)
        gather(FAR, 1, 3 * blk)

        @both_chunks
        def _(columns):
            fold(1, columns, 2 * blk, near_highs)

    @when(inner == 1)
    def _():
        pass_theirs()
        for i, slot in enumerate((NEAR, FAR)):
            gather(slot, 0, i * blk)
            gather(slot, 1, (2 + i) * blk)

        @both_chunks
        def _(columns):
            fold(1, columns, 0, [None, None] + near_highs)
            fold(0, columns, 0, near_lows)

    @when(inner == 0)
    def _():
        pass_mine(False)

    arrived(WIDE, 0)
    arrived(WIDE, 1)
    gather(WIDE, 0, 0)
    gather(WIDE, 1, blk)

    @both_chunks
    def _(columns):
        fold(1, columns, 0, [None, high_hide(wide)])
        fold(0, columns, 0, [low_hide(wide)])

    @when(inner == 0)
    def _():
        when(mine == 0)(low_unit)
        when(mine == 1)(high_unit)
        pass_theirs()
        when(mine == 0)(high_unit)
        when(mine == 1)(low_unit)

    for h in range(heads):
        for b in range(2):
            columns = pl.ds(h * blk, blk)
            o_lat = (acc[b, :, columns] * (1.0 / sum_s[b, :1, columns])).astype(jnp.bfloat16)
            out_ref[h, pl.ds(b * blk, blk), :] = jnp.dot(
                o_lat.T, wuv[h], preferred_element_type=jnp.float32
            ).astype(jnp.bfloat16)
    for copy in own + mirrored + forward:
        copy.wait_send()

    @when(inner == 1)
    def _():
        for copy in relays:
            copy.wait_send()


def per_device(q_nope, q_rope, c_kv, k_rope, block_pos, w_uk, w_uv):
    rows, heads, nope = q_nope.shape
    blk = rows // 2
    lat = c_kv.shape[1]
    rope = k_rope.shape[1]
    factor = math.log2(math.e) / math.sqrt(nope + rope)
    vmem = pl.BlockSpec(memory_space=pltpu.VMEM)
    anywhere = pl.BlockSpec(memory_space=pltpu.HBM)
    bf16, f32 = jnp.bfloat16, jnp.float32
    out = pl.pallas_call(
        functools.partial(attention_kernel, factor),
        out_shape=jax.ShapeDtypeStruct((heads, rows, w_uv.shape[2]), bf16),
        in_specs=[pl.BlockSpec(memory_space=pltpu.SMEM)] + [anywhere] * 6,
        out_specs=vmem,
        scratch_shapes=[
            pltpu.VMEM(c_kv.shape, bf16),
            pltpu.VMEM((rope, rows), bf16),
            pltpu.VMEM(q_nope.shape, bf16),
            pltpu.VMEM((heads, rope, rows), bf16),
            pltpu.VMEM(w_uk.shape, bf16),
            pltpu.VMEM(w_uv.shape, bf16),
            pltpu.VMEM((rows * heads, nope), f32),
            pltpu.VMEM((2, lat + 2 * rope, blk * heads), bf16),
            pltpu.VMEM((5, 2, 9, blk // 2, LANES), bf16),
            pltpu.VMEM((4 * blk, lat + 2 * rope), bf16),
            pltpu.VMEM((lat, 4 * blk), bf16),
            pltpu.VMEM((2, lat, blk * heads), f32),
            pltpu.VMEM((2, 8, blk * heads), f32),
            pltpu.VMEM((2, 8, blk * heads), f32),
            pltpu.VMEM((blk, blk), f32),
            pltpu.SemaphoreType.DMA((6,)),
            pltpu.SemaphoreType.DMA((9,)),
            pltpu.SemaphoreType.DMA((4, 2)),
        ],
        compiler_params=pltpu.CompilerParams(
            collective_id=0, has_side_effects=True, vmem_limit_bytes=60 * 1024 * 1024
        ),
        cost_estimate=pl.CostEstimate(
            flops=6 * 10**9, bytes_accessed=5 * 10**6, transcendentals=2 * 10**6
        ),
    )(block_pos, c_kv, k_rope.T, q_nope, jnp.transpose(q_rope, (1, 2, 0)), w_uk, w_uv)
    return jnp.transpose(out, (1, 0, 2))


def solution(mesh):
    placed = (
        P("ctx", "head", None),
        P("ctx", "head", None),
        P("ctx", None),
        P("ctx", None),
        P(),
        P("head", None, None),
        P("head", None, None),
    )
    return jax.shard_map(
        per_device, mesh=mesh, in_specs=placed, out_specs=P("ctx", "head", None), check_vma=False
    )
```

```python
import functools
import math

import jax
import jax.numpy as jnp
from jax import lax
from jax.experimental import pallas as pl
from jax.experimental.pallas import tpu as pltpu
from jax.sharding import PartitionSpec as P

MESH = pl.DeviceIdType.MESH
LANES = 128
PIECES = ((0, 3), (3, 2), (5, 2), (7, 2))
PARTNER, NEAR, FAR, WIDE = 0, 1, 2, 3


def attention_kernel(
    factor,
    pos_ref, ckv_hbm, krope_hbm, qn_hbm, qr_hbm, wuk_hbm, wuv_hbm, out_ref,
    ckv_ref, krope_ref, qn, qr, wuk, wuv, flat, qs, held, keys, values, acc, top_s, sum_s, wall,
    load_sem, send_sem, recv_sem,
):
    n = lax.axis_size("ctx")
    me = lax.axis_index("ctx")
    heads = qn.shape[1]
    blk = ckv_ref.shape[0] // 2
    lat = ckv_ref.shape[1]
    rope = krope_ref.shape[0]
    core = lax.rem(me, 2)
    side = lax.rem(lax.div(me, 2), 2)
    inner = lax.rem(core + side, 2)
    toward = 1 - 2 * side

    def at(by):
        return lax.rem(me + by + n, n)

    partner = at(1 - 2 * core)
    near = at(2 * core - 1)
    far = at(4 * core - 2)
    wide = at(2 - 4 * core)
    across = at(2 * toward)
    relay = at(3 * toward * (2 * inner - 1))

    loads = [
        pltpu.make_async_copy(a, b, load_sem.at[i])
        for i, (a, b) in enumerate(
            ((ckv_hbm, ckv_ref), (krope_hbm, krope_ref), (qn_hbm, qn),
             (wuk_hbm, wuk), (qr_hbm, qr), (wuv_hbm, wuv))
        )
    ]
    for load in loads:
        load.start()

    barrier = pltpu.get_barrier_semaphore()
    for other in (partner, near, across, relay):
        pl.semaphore_signal(barrier, inc=1, device_id={"ctx": other}, device_id_type=MESH)

    loads[0].wait()
    loads[1].wait()
    for c in range(4):
        held[4, c] = ckv_ref[:blk, c * LANES:(c + 1) * LANES]
        held[4, 5 + c] = ckv_ref[blk:, c * LANES:(c + 1) * LANES]
    held[4, 4, :, :rope] = krope_ref[:, :blk].T
    held[4, 4, :, rope:] = krope_ref[:, blk:].T
    pl.semaphore_wait(barrier, 4)

    def send(slot_from, slot_to, piece, target, flag=None):
        start, size = PIECES[piece]
        return pltpu.make_async_remote_copy(
            src_ref=held.at[slot_from, pl.ds(start, size)],
            dst_ref=held.at[slot_to, pl.ds(start, size)],
            send_sem=send_sem.at[slot_to if flag is None else flag, piece],
            recv_sem=recv_sem.at[slot_to, piece],
            device_id={"ctx": target},
            device_id_type=MESH,
        )

    def arrived(slot, piece):
        send(slot, slot, piece, partner).wait_recv()

    own = []
    for piece in range(len(PIECES)):
        own.append(send(4, 2 - inner, piece, at(toward * (2 - inner))))
        own.append(send(4, PARTNER, piece, partner))
    for copy in own:
        copy.start()
    forward = [send(NEAR, WIDE, piece, partner) for piece in range(len(PIECES))]
    relays = [
        send(a, b, piece, relay, flag)
        for piece in range(len(PIECES))
        for a, b, flag in ((FAR, NEAR, 4), (NEAR, FAR, FAR))
    ]

    def pass_on(piece):
        arrived(FAR, piece)
        relays[2 * piece].start()
        arrived(NEAR, piece)
        relays[2 * piece + 1].start()
        forward[piece].start()

    loads[2].wait()
    flat[...] = qn[...].astype(jnp.float32).reshape(flat.shape)
    loads[3].wait()
    loads[4].wait()
    for h in range(heads):
        part = flat[pl.ds(h, 2 * blk, stride=heads), :].astype(jnp.bfloat16)
        turned = lax.dot_general(
            wuk[h], part, (((0,), (1,)), ((), ())), preferred_element_type=jnp.float32
        ).astype(jnp.bfloat16)
        for b in range(2):
            into = pl.ds(h * blk, blk)
            qs[b, :lat, into] = turned[:, b * blk:(b + 1) * blk]
            rotary = qr[h, :, b * blk:(b + 1) * blk]
            qs[b, lat:lat + rope, into] = rotary
            qs[b, lat + rope:, into] = rotary

    my_pos = pos_ref[2 * me]
    lane = lax.broadcasted_iota(jnp.int32, (blk, LANES), 1)
    wall[...] = jnp.where(
        lax.broadcasted_iota(jnp.int32, (blk, blk), 0)
        <= lax.broadcasted_iota(jnp.int32, (blk, blk), 1),
        0.0,
        -1e30,
    )
    chunk = qs.shape[2] // 4

    def gather_low(slot, base):
        for c in range(4):
            piece = held[slot, c]
            keys[pl.ds(base, blk), c * LANES:(c + 1) * LANES] = piece
            values[c * LANES:(c + 1) * LANES, pl.ds(base, blk)] = piece.T
        both = held[slot, 4]
        keys[pl.ds(base, blk), lat:] = jnp.where(lane < rope, both, jnp.zeros_like(both))

    def gather_high(slot, base):
        for c in range(4):
            piece = held[slot, 5 + c]
            keys[pl.ds(base, blk), c * LANES:(c + 1) * LANES] = piece
            values[c * LANES:(c + 1) * LANES, pl.ds(base, blk)] = piece.T
        both = held[slot, 4]
        keys[pl.ds(base, blk), lat:] = jnp.where(lane < rope, jnp.zeros_like(both), both)

    def score_of(task):
        b, columns, base, hides, first = task
        rows = pl.ds(base, len(hides) * blk)
        return jnp.dot(keys[rows, :], qs[b, :, columns], preferred_element_type=jnp.float32)

    def fold(task, score):
        b, columns, base, hides, first = task
        rows = pl.ds(base, len(hides) * blk)
        score = score * factor
        parts = []
        for i, hide in enumerate(hides):
            part = score[i * blk:(i + 1) * blk]
            if hide is wall:
                part = part + jnp.concatenate([wall[...]] * (chunk // blk), axis=1)
            elif hide is not None:
                part = part + hide
            parts.append(part)
        best = functools.reduce(jnp.maximum, parts)
        best = jnp.max(best, axis=0, keepdims=True)
        if not first:
            old = top_s[b, :1, columns]
            best = jnp.maximum(best, old)
        parts = [jnp.exp2(part - best) for part in parts]
        total = jnp.sum(functools.reduce(jnp.add, parts), axis=0, keepdims=True)
        weights = jnp.concatenate([part.astype(jnp.bfloat16) for part in parts], axis=0)
        mixed = jnp.dot(values[:, rows], weights, preferred_element_type=jnp.float32)
        if not first:
            shrink = jnp.exp2(old - best)
            total = total + sum_s[b, :1, columns] * shrink
            mixed = mixed + acc[b, :, columns] * shrink
        acc[b, :, columns] = mixed
        top_s[b, :1, columns] = best
        sum_s[b, :1, columns] = total

    def run(tasks):
        ahead = score_of(tasks[0])
        for i, task in enumerate(tasks):
            score = ahead
            if i + 1 < len(tasks):
                ahead = score_of(tasks[i + 1])
            fold(task, score)

    def in_pairs(units):
        def step(c, carry):
            run([
                (b, pl.ds(pl.multiple_of((2 * c + i) * chunk, chunk), chunk), base, hides, False)
                for b, base, hides in units
                for i in range(2)
            ])
            return carry

        lax.fori_loop(0, 2, step, 0)

    def low_hide(source):
        return jnp.where(pos_ref[2 * source] <= my_pos, 0.0, -1e30)

    def high_hide(source):
        return jnp.where(pos_ref[2 * source] >= my_pos, 0.0, -1e30)

    def inner_passes(piece):
        @pl.when(inner == 1)
        def _():
            pass_on(piece)

    def outer_passes(piece):
        @pl.when(inner == 0)
        def _():
            arrived(NEAR, piece)
            forward[piece].start()

    loads[5].wait()
    inner_passes(0)
    for piece in range(len(PIECES)):
        arrived(PARTNER, piece)
    gather_low(4, 0)
    gather_low(PARTNER, blk)
    gather_high(4, 2 * blk)
    gather_high(PARTNER, 3 * blk)
    lows, highs = [wall, low_hide(partner)], [wall, high_hide(partner)]
    run([(1, pl.ds(c * chunk, chunk), 0, [None, None] + highs, True) for c in range(4)])
    inner_passes(1)
    run([(0, pl.ds(c * chunk, chunk), 0, lows, True) for c in range(4)])
    inner_passes(2)
    inner_passes(3)

    near_lows, near_highs = [low_hide(near), low_hide(far)], [high_hide(near), high_hide(far)]

    @pl.when(inner == 1)
    def _():
        gather_low(NEAR, 0)
        gather_low(FAR, blk)
        gather_high(NEAR, 2 * blk)
        gather_high(FAR, 3 * blk)

        in_pairs([(1, 0, [None, None] + near_highs), (0, 0, near_lows)])

    outer_passes(0)
    arrived(WIDE, 0)
    arrived(WIDE, 1)
    gather_low(WIDE, 0)

    in_pairs([(1, 0, [None]), (0, 0, [low_hide(wide)])])

    outer_passes(1)
    arrived(WIDE, 2)
    arrived(WIDE, 3)
    gather_high(WIDE, blk)

    in_pairs([(1, blk, [high_hide(wide)])])

    @pl.when(inner == 0)
    def _():
        arrived(FAR, 0)
        arrived(FAR, 1)
        gather_low(NEAR, 0)
        gather_low(FAR, blk)

        in_pairs([(1, 0, [None, None]), (0, 0, near_lows)])

    outer_passes(2)
    outer_passes(3)

    @pl.when(inner == 0)
    def _():
        arrived(FAR, 2)
        arrived(FAR, 3)
        gather_high(NEAR, 2 * blk)
        gather_high(FAR, 3 * blk)

        in_pairs([(1, 2 * blk, near_highs)])

    for h in range(heads):
        for b in range(2):
            columns = pl.ds(h * blk, blk)
            o_lat = (acc[b, :, columns] * (1.0 / sum_s[b, :1, columns])).astype(jnp.bfloat16)
            flat[pl.ds(b * blk * heads + h, blk, stride=heads), :] = jnp.dot(
                o_lat.T, wuv[h], preferred_element_type=jnp.float32
            )
    out_ref[...] = flat[...].reshape(out_ref.shape).astype(jnp.bfloat16)
    for copy in own + forward:
        copy.wait_send()

    @pl.when(inner == 1)
    def _():
        for copy in relays:
            copy.wait_send()


def per_device(q_nope, q_rope, c_kv, k_rope, block_pos, w_uk, w_uv):
    rows, heads, nope = q_nope.shape
    blk = rows // 2
    lat = c_kv.shape[1]
    rope = k_rope.shape[1]
    factor = math.log2(math.e) / math.sqrt(nope + rope)
    vmem = pl.BlockSpec(memory_space=pltpu.VMEM)
    anywhere = pl.BlockSpec(memory_space=pltpu.HBM)
    bf16, f32 = jnp.bfloat16, jnp.float32
    return pl.pallas_call(
        functools.partial(attention_kernel, factor),
        out_shape=jax.ShapeDtypeStruct((rows, heads, w_uv.shape[2]), bf16),
        in_specs=[pl.BlockSpec(memory_space=pltpu.SMEM)] + [anywhere] * 6,
        out_specs=vmem,
        scratch_shapes=[
            pltpu.VMEM(c_kv.shape, bf16),
            pltpu.VMEM((rope, rows), bf16),
            pltpu.VMEM(q_nope.shape, bf16),
            pltpu.VMEM((heads, rope, rows), bf16),
            pltpu.VMEM(w_uk.shape, bf16),
            pltpu.VMEM(w_uv.shape, bf16),
            pltpu.VMEM((rows * heads, nope), f32),
            pltpu.VMEM((2, lat + 2 * rope, blk * heads), bf16),
            pltpu.VMEM((5, 9, blk, LANES), bf16),
            pltpu.VMEM((4 * blk, lat + 2 * rope), bf16),
            pltpu.VMEM((lat, 4 * blk), bf16),
            pltpu.VMEM((2, lat, blk * heads), f32),
            pltpu.VMEM((2, 8, blk * heads), f32),
            pltpu.VMEM((2, 8, blk * heads), f32),
            pltpu.VMEM((blk, blk), f32),
            pltpu.SemaphoreType.DMA((6,)),
            pltpu.SemaphoreType.DMA((5, len(PIECES))),
            pltpu.SemaphoreType.DMA((4, len(PIECES))),
        ],
        compiler_params=pltpu.CompilerParams(
            collective_id=0, has_side_effects=True, vmem_limit_bytes=60 * 1024 * 1024
        ),
        cost_estimate=pl.CostEstimate(
            flops=6 * 10**9, bytes_accessed=5 * 10**6, transcendentals=2 * 10**6
        ),
    )(block_pos, c_kv, k_rope.T, q_nope, jnp.transpose(q_rope, (1, 2, 0)), w_uk, w_uv)


def solution(mesh):
    placed = (
        P("ctx", "head", None),
        P("ctx", "head", None),
        P("ctx", None),
        P("ctx", None),
        P(),
        P("head", None, None),
        P("head", None, None),
    )
    return jax.shard_map(
        per_device, mesh=mesh, in_specs=placed, out_specs=P("ctx", "head", None), check_vma=False
    )
```

```python
import functools
import math

import jax
import jax.numpy as jnp
from jax import lax
from jax.experimental import pallas as pl
from jax.experimental.pallas import tpu as pltpu
from jax.sharding import PartitionSpec as P

MESH = pl.DeviceIdType.MESH
LANES = 128
PIECES = ((0, 3), (3, 2), (5, 2), (7, 2))
PARTNER, NEAR, FAR, WIDE = 0, 1, 2, 3


def attention_kernel(
    factor,
    pos_ref, ckv_hbm, krope_hbm, qn_hbm, qr_hbm, wuk_hbm, wuv_hbm, out_ref,
    ckv_ref, krope_ref, qn, qr, wuk, wuv, flat, qs, held, keys, values, acc, top_s, sum_s, wall,
    load_sem, send_sem, recv_sem,
):
    n = lax.axis_size("ctx")
    me = lax.axis_index("ctx")
    heads = qn.shape[1]
    blk = ckv_ref.shape[0] // 2
    lat = ckv_ref.shape[1]
    rope = krope_ref.shape[0]
    core = lax.rem(me, 2)
    side = lax.rem(lax.div(me, 2), 2)
    inner = lax.rem(core + side, 2)
    toward = 1 - 2 * side

    def at(by):
        return lax.rem(me + by + n, n)

    partner = at(1 - 2 * core)
    near = at(2 * core - 1)
    far = at(4 * core - 2)
    wide = at(2 - 4 * core)
    across = at(2 * toward)
    relay = at(3 * toward * (2 * inner - 1))

    loads = [
        pltpu.make_async_copy(a, b, load_sem.at[i])
        for i, (a, b) in enumerate(
            ((ckv_hbm, ckv_ref), (krope_hbm, krope_ref), (qn_hbm, qn),
             (wuk_hbm, wuk), (qr_hbm, qr), (wuv_hbm, wuv))
        )
    ]
    for load in loads:
        load.start()

    barrier = pltpu.get_barrier_semaphore()
    for other in (partner, near, across, relay):
        pl.semaphore_signal(barrier, inc=1, device_id={"ctx": other}, device_id_type=MESH)

    loads[0].wait()
    loads[1].wait()
    for c in range(4):
        held[4, c] = ckv_ref[:blk, c * LANES:(c + 1) * LANES]
        held[4, 5 + c] = ckv_ref[blk:, c * LANES:(c + 1) * LANES]
    held[4, 4, :, :rope] = krope_ref[:, :blk].T
    held[4, 4, :, rope:] = krope_ref[:, blk:].T
    pl.semaphore_wait(barrier, 4)

    def send(slot_from, slot_to, piece, target, flag=None):
        start, size = PIECES[piece]
        return pltpu.make_async_remote_copy(
            src_ref=held.at[slot_from, pl.ds(start, size)],
            dst_ref=held.at[slot_to, pl.ds(start, size)],
            send_sem=send_sem.at[slot_to if flag is None else flag, piece],
            recv_sem=recv_sem.at[slot_to, piece],
            device_id={"ctx": target},
            device_id_type=MESH,
        )

    def arrived(slot, piece):
        send(slot, slot, piece, partner).wait_recv()

    own = []
    for piece in range(len(PIECES)):
        own.append(send(4, 2 - inner, piece, at(toward * (2 - inner))))
        own.append(send(4, PARTNER, piece, partner))
    for copy in own:
        copy.start()
    forward = [send(NEAR, WIDE, piece, partner) for piece in range(len(PIECES))]
    relays = [
        send(a, b, piece, relay, flag)
        for piece in range(len(PIECES))
        for a, b, flag in ((FAR, NEAR, 4), (NEAR, FAR, FAR))
    ]

    def pass_on(piece):
        arrived(FAR, piece)
        relays[2 * piece].start()
        arrived(NEAR, piece)
        relays[2 * piece + 1].start()
        forward[piece].start()

    loads[2].wait()
    flat[...] = qn[...].astype(jnp.float32).reshape(flat.shape)
    loads[3].wait()
    loads[4].wait()
    for h in range(heads):
        part = flat[pl.ds(h, 2 * blk, stride=heads), :].astype(jnp.bfloat16)
        turned = lax.dot_general(
            wuk[h], part, (((0,), (1,)), ((), ())), preferred_element_type=jnp.float32
        ).astype(jnp.bfloat16)
        for b in range(2):
            into = pl.ds(h * blk, blk)
            qs[b, :lat, into] = turned[:, b * blk:(b + 1) * blk]
            rotary = qr[h, :, b * blk:(b + 1) * blk]
            qs[b, lat:lat + rope, into] = rotary
            qs[b, lat + rope:, into] = rotary

    my_pos = pos_ref[2 * me]
    lane = lax.broadcasted_iota(jnp.int32, (blk, LANES), 1)
    wall[...] = jnp.where(
        lax.broadcasted_iota(jnp.int32, (blk, blk), 0)
        <= lax.broadcasted_iota(jnp.int32, (blk, blk), 1),
        0.0,
        -1e30,
    )
    chunk = qs.shape[2] // 2

    def gather_low(slot, base):
        for c in range(4):
            piece = held[slot, c]
            keys[pl.ds(base, blk), c * LANES:(c + 1) * LANES] = piece
            values[c * LANES:(c + 1) * LANES, pl.ds(base, blk)] = piece.T
        both = held[slot, 4]
        keys[pl.ds(base, blk), lat:] = jnp.where(lane < rope, both, jnp.zeros_like(both))

    def gather_high(slot, base):
        for c in range(4):
            piece = held[slot, 5 + c]
            keys[pl.ds(base, blk), c * LANES:(c + 1) * LANES] = piece
            values[c * LANES:(c + 1) * LANES, pl.ds(base, blk)] = piece.T
        both = held[slot, 4]
        keys[pl.ds(base, blk), lat:] = jnp.where(lane < rope, jnp.zeros_like(both), both)

    def fold(b, columns, base, hides, first=False):
        rows = pl.ds(base, len(hides) * blk)
        score = jnp.dot(
            keys[rows, :], qs[b, :, columns], preferred_element_type=jnp.float32
        ) * factor
        parts = []
        for i, hide in enumerate(hides):
            part = score[i * blk:(i + 1) * blk]
            if hide is wall:
                part = part + jnp.concatenate([wall[...]] * (chunk // blk), axis=1)
            elif hide is not None:
                part = part + hide
            parts.append(part)
        best = functools.reduce(jnp.maximum, parts)
        best = jnp.max(best, axis=0, keepdims=True)
        if not first:
            old = top_s[b, :1, columns]
            best = jnp.maximum(best, old)
        parts = [jnp.exp2(part - best) for part in parts]
        total = jnp.sum(functools.reduce(jnp.add, parts), axis=0, keepdims=True)
        weights = jnp.concatenate([part.astype(jnp.bfloat16) for part in parts], axis=0)
        mixed = jnp.dot(values[:, rows], weights, preferred_element_type=jnp.float32)
        if not first:
            shrink = jnp.exp2(old - best)
            total = total + sum_s[b, :1, columns] * shrink
            mixed = mixed + acc[b, :, columns] * shrink
        acc[b, :, columns] = mixed
        top_s[b, :1, columns] = best
        sum_s[b, :1, columns] = total

    def part_of(c):
        return pl.ds(c * chunk if isinstance(c, int) else pl.multiple_of(c * chunk, chunk), chunk)

    def both_chunks(body):
        def step(c, carry):
            body(part_of(c))
            return carry

        lax.fori_loop(0, 2, step, 0)

    def low_hide(source):
        return jnp.where(pos_ref[2 * source] <= my_pos, 0.0, -1e30)

    def high_hide(source):
        return jnp.where(pos_ref[2 * source] >= my_pos, 0.0, -1e30)

    def inner_passes(piece):
        @pl.when(inner == 1)
        def _():
            pass_on(piece)

    def outer_passes(piece):
        @pl.when(inner == 0)
        def _():
            arrived(NEAR, piece)
            forward[piece].start()

    loads[5].wait()
    inner_passes(0)
    inner_passes(1)
    for piece in range(len(PIECES)):
        arrived(PARTNER, piece)
    gather_low(4, 0)
    gather_low(PARTNER, blk)
    gather_high(4, 2 * blk)
    gather_high(PARTNER, 3 * blk)
    lows, highs = [wall, low_hide(partner)], [wall, high_hide(partner)]
    fold(1, part_of(0), 0, [None, None] + highs, True)
    fold(0, part_of(0), 0, lows, True)
    inner_passes(2)
    fold(1, part_of(1), 0, [None, None] + highs, True)
    inner_passes(3)
    fold(0, part_of(1), 0, lows, True)

    near_lows, near_highs = [low_hide(near), low_hide(far)], [high_hide(near), high_hide(far)]

    @pl.when(inner == 1)
    def _():
        gather_low(NEAR, 0)
        gather_low(FAR, blk)
        gather_high(NEAR, 2 * blk)
        gather_high(FAR, 3 * blk)

        @both_chunks
        def _(columns):
            fold(1, columns, 0, [None, None] + near_highs)
            fold(0, columns, 0, near_lows)

    outer_passes(0)
    arrived(WIDE, 0)
    arrived(WIDE, 1)
    gather_low(WIDE, 0)

    @both_chunks
    def _(columns):
        fold(1, columns, 0, [None])
        fold(0, columns, 0, [low_hide(wide)])

    outer_passes(1)
    arrived(WIDE, 2)
    arrived(WIDE, 3)
    gather_high(WIDE, blk)

    @both_chunks
    def _(columns):
        fold(1, columns, blk, [high_hide(wide)])

    @pl.when(inner == 0)
    def _():
        arrived(FAR, 0)
        arrived(FAR, 1)
        gather_low(NEAR, 0)
        gather_low(FAR, blk)

        @both_chunks
        def _(columns):
            fold(1, columns, 0, [None, None])
            fold(0, columns, 0, near_lows)

    outer_passes(2)
    outer_passes(3)

    @pl.when(inner == 0)
    def _():
        arrived(FAR, 2)
        arrived(FAR, 3)
        gather_high(NEAR, 2 * blk)
        gather_high(FAR, 3 * blk)

        @both_chunks
        def _(columns):
            fold(1, columns, 2 * blk, near_highs)

    for h in range(heads):
        for b in range(2):
            columns = pl.ds(h * blk, blk)
            o_lat = (acc[b, :, columns] * (1.0 / sum_s[b, :1, columns])).astype(jnp.bfloat16)
            flat[pl.ds(b * blk * heads + h, blk, stride=heads), :] = jnp.dot(
                o_lat.T, wuv[h], preferred_element_type=jnp.float32
            )
    out_ref[...] = flat[...].reshape(out_ref.shape).astype(jnp.bfloat16)
    for copy in own + forward:
        copy.wait_send()

    @pl.when(inner == 1)
    def _():
        for copy in relays:
            copy.wait_send()


def per_device(q_nope, q_rope, c_kv, k_rope, block_pos, w_uk, w_uv):
    rows, heads, nope = q_nope.shape
    blk = rows // 2
    lat = c_kv.shape[1]
    rope = k_rope.shape[1]
    factor = math.log2(math.e) / math.sqrt(nope + rope)
    vmem = pl.BlockSpec(memory_space=pltpu.VMEM)
    anywhere = pl.BlockSpec(memory_space=pltpu.HBM)
    bf16, f32 = jnp.bfloat16, jnp.float32
    return pl.pallas_call(
        functools.partial(attention_kernel, factor),
        out_shape=jax.ShapeDtypeStruct((rows, heads, w_uv.shape[2]), bf16),
        in_specs=[pl.BlockSpec(memory_space=pltpu.SMEM)] + [anywhere] * 6,
        out_specs=vmem,
        scratch_shapes=[
            pltpu.VMEM(c_kv.shape, bf16),
            pltpu.VMEM((rope, rows), bf16),
            pltpu.VMEM(q_nope.shape, bf16),
            pltpu.VMEM((heads, rope, rows), bf16),
            pltpu.VMEM(w_uk.shape, bf16),
            pltpu.VMEM(w_uv.shape, bf16),
            pltpu.VMEM((rows * heads, nope), f32),
            pltpu.VMEM((2, lat + 2 * rope, blk * heads), bf16),
            pltpu.VMEM((5, 9, blk, LANES), bf16),
            pltpu.VMEM((4 * blk, lat + 2 * rope), bf16),
            pltpu.VMEM((lat, 4 * blk), bf16),
            pltpu.VMEM((2, lat, blk * heads), f32),
            pltpu.VMEM((2, 8, blk * heads), f32),
            pltpu.VMEM((2, 8, blk * heads), f32),
            pltpu.VMEM((blk, blk), f32),
            pltpu.SemaphoreType.DMA((6,)),
            pltpu.SemaphoreType.DMA((5, len(PIECES))),
            pltpu.SemaphoreType.DMA((4, len(PIECES))),
        ],
        compiler_params=pltpu.CompilerParams(
            collective_id=0, has_side_effects=True, vmem_limit_bytes=60 * 1024 * 1024
        ),
        cost_estimate=pl.CostEstimate(
            flops=6 * 10**9, bytes_accessed=5 * 10**6, transcendentals=2 * 10**6
        ),
    )(block_pos, c_kv, k_rope.T, q_nope, jnp.transpose(q_rope, (1, 2, 0)), w_uk, w_uv)


def solution(mesh):
    placed = (
        P("ctx", "head", None),
        P("ctx", "head", None),
        P("ctx", None),
        P("ctx", None),
        P(),
        P("head", None, None),
        P("head", None, None),
    )
    return jax.shard_map(
        per_device, mesh=mesh, in_specs=placed, out_specs=P("ctx", "head", None), check_vma=False
    )
```

```python
import functools
import math

import jax
import jax.numpy as jnp
from jax import lax
from jax.experimental import pallas as pl
from jax.experimental.pallas import tpu as pltpu
from jax.sharding import PartitionSpec as P

MESH = pl.DeviceIdType.MESH
LANES = 128
PIECES = ((0, 3), (3, 2), (5, 2), (7, 2))
PARTNER, NEAR, FAR, WIDE = 0, 1, 2, 3


def attention_kernel(
    factor,
    pos_ref, ckv_hbm, krope_hbm, qn_hbm, qr_hbm, wuk_hbm, wuv_hbm, out_ref,
    ckv_ref, krope_ref, qn, qr, wuk, wuv, flat, qs, held, keys, values, acc, top_s, sum_s, wall,
    load_sem, send_sem, recv_sem,
):
    n = lax.axis_size("ctx")
    me = lax.axis_index("ctx")
    heads = qn.shape[1]
    blk = ckv_ref.shape[0] // 2
    lat = ckv_ref.shape[1]
    rope = krope_ref.shape[0]
    core = lax.rem(me, 2)
    side = lax.rem(lax.div(me, 2), 2)
    inner = lax.rem(core + side, 2)
    toward = 1 - 2 * side

    def at(by):
        return lax.rem(me + by + n, n)

    partner = at(1 - 2 * core)
    near = at(2 * core - 1)
    far = at(4 * core - 2)
    wide = at(2 - 4 * core)
    across = at(2 * toward)
    relay = at(3 * toward * (2 * inner - 1))

    loads = [
        pltpu.make_async_copy(a, b, load_sem.at[i])
        for i, (a, b) in enumerate(
            ((ckv_hbm, ckv_ref), (krope_hbm, krope_ref), (qn_hbm, qn),
             (wuk_hbm, wuk), (qr_hbm, qr), (wuv_hbm, wuv))
        )
    ]
    for load in loads:
        load.start()

    barrier = pltpu.get_barrier_semaphore()
    for other in (partner, near, across, relay, at(4), at(-4)):
        pl.semaphore_signal(barrier, inc=1, device_id={"ctx": other}, device_id_type=MESH)

    loads[0].wait()
    loads[1].wait()
    for c in range(4):
        held[4, c] = ckv_ref[:blk, c * LANES:(c + 1) * LANES]
        held[4, 5 + c] = ckv_ref[blk:, c * LANES:(c + 1) * LANES]
    held[4, 4, :, :rope] = krope_ref[:, :blk].T
    held[4, 4, :, rope:] = krope_ref[:, blk:].T
    pl.semaphore_wait(barrier, 6)

    def send(slot_from, slot_to, piece, target, flag=None):
        start, size = PIECES[piece]
        return pltpu.make_async_remote_copy(
            src_ref=held.at[slot_from, pl.ds(start, size)],
            dst_ref=held.at[slot_to, pl.ds(start, size)],
            send_sem=send_sem.at[slot_to if flag is None else flag, piece],
            recv_sem=recv_sem.at[slot_to, piece],
            device_id={"ctx": target},
            device_id_type=MESH,
        )

    def arrived(slot, piece):
        send(slot, slot, piece, partner).wait_recv()

    own = []
    for piece in range(len(PIECES)):
        own.append(send(4, 2 - inner, piece, at(toward * (2 - inner))))
        own.append(send(4, PARTNER, piece, partner))
    for copy in own:
        copy.start()
    forward = [send(NEAR, WIDE, piece, partner) for piece in range(len(PIECES))]
    relays = [
        send(a, b, piece, relay, flag)
        for piece in range(len(PIECES))
        for a, b, flag in ((FAR, NEAR, 4), (NEAR, FAR, FAR))
    ]
    onward = [send(FAR, WIDE, piece, at(4 * toward), 5) for piece in range(len(PIECES))]

    def pass_on(piece):
        arrived(FAR, piece)
        relays[2 * piece].start()
        onward[piece].start()
        arrived(NEAR, piece)
        relays[2 * piece + 1].start()
        forward[piece].start()

    loads[2].wait()
    flat[...] = qn[...].astype(jnp.float32).reshape(flat.shape)
    loads[3].wait()
    loads[4].wait()
    for h in range(heads):
        part = flat[pl.ds(h, 2 * blk, stride=heads), :].astype(jnp.bfloat16)
        turned = jnp.dot(part, wuk[h], preferred_element_type=jnp.float32).astype(jnp.bfloat16).T
        for b in range(2):
            into = pl.ds(h * blk, blk)
            qs[b, :lat, into] = turned[:, b * blk:(b + 1) * blk]
            rotary = qr[h, :, b * blk:(b + 1) * blk]
            qs[b, lat:lat + rope, into] = rotary
            qs[b, lat + rope:, into] = rotary

    my_pos = pos_ref[2 * me]
    lane = lax.broadcasted_iota(jnp.int32, (blk, LANES), 1)
    wall[...] = jnp.where(
        lax.broadcasted_iota(jnp.int32, (blk, blk), 0)
        <= lax.broadcasted_iota(jnp.int32, (blk, blk), 1),
        0.0,
        -1e30,
    )
    chunk = qs.shape[2] // 2

    def gather_low(slot, base):
        for c in range(4):
            piece = held[slot, c]
            keys[pl.ds(base, blk), c * LANES:(c + 1) * LANES] = piece
            values[c * LANES:(c + 1) * LANES, pl.ds(base, blk)] = piece.T
        both = held[slot, 4]
        keys[pl.ds(base, blk), lat:] = jnp.where(lane < rope, both, jnp.zeros_like(both))

    def gather_high(slot, base):
        for c in range(4):
            piece = held[slot, 5 + c]
            keys[pl.ds(base, blk), c * LANES:(c + 1) * LANES] = piece
            values[c * LANES:(c + 1) * LANES, pl.ds(base, blk)] = piece.T
        both = held[slot, 4]
        keys[pl.ds(base, blk), lat:] = jnp.where(lane < rope, jnp.zeros_like(both), both)

    def fold(b, columns, base, hides, first=False):
        rows = pl.ds(base, len(hides) * blk)
        score = jnp.dot(
            keys[rows, :], qs[b, :, columns], preferred_element_type=jnp.float32
        ) * factor
        parts = []
        for i, hide in enumerate(hides):
            part = score[i * blk:(i + 1) * blk]
            if hide is wall:
                part = part + jnp.concatenate([wall[...]] * (chunk // blk), axis=1)
            elif hide is not None:
                part = part + hide
            parts.append(part)
        best = functools.reduce(jnp.maximum, parts)
        best = jnp.max(best, axis=0, keepdims=True)
        if not first:
            old = top_s[b, :1, columns]
            best = jnp.maximum(best, old)
        parts = [jnp.exp2(part - best) for part in parts]
        total = jnp.sum(functools.reduce(jnp.add, parts), axis=0, keepdims=True)
        weights = jnp.concatenate([part.astype(jnp.bfloat16) for part in parts], axis=0)
        mixed = jnp.dot(values[:, rows], weights, preferred_element_type=jnp.float32)
        if not first:
            shrink = jnp.exp2(old - best)
            total = total + sum_s[b, :1, columns] * shrink
            mixed = mixed + acc[b, :, columns] * shrink
        acc[b, :, columns] = mixed
        top_s[b, :1, columns] = best
        sum_s[b, :1, columns] = total

    def part_of(c):
        return pl.ds(c * chunk if isinstance(c, int) else pl.multiple_of(c * chunk, chunk), chunk)

    def both_chunks(body):
        def step(c, carry):
            body(part_of(c))
            return carry

        lax.fori_loop(0, 2, step, 0)

    def low_hide(source):
        return jnp.where(pos_ref[2 * source] <= my_pos, 0.0, -1e30)

    def high_hide(source):
        return jnp.where(pos_ref[2 * source] >= my_pos, 0.0, -1e30)

    def inner_passes(piece):
        @pl.when(inner == 1)
        def _():
            pass_on(piece)

    def outer_passes(piece):
        @pl.when(inner == 0)
        def _():
            arrived(NEAR, piece)

    loads[5].wait()
    inner_passes(0)
    for piece in range(len(PIECES)):
        arrived(PARTNER, piece)
    gather_low(4, 0)
    gather_low(PARTNER, blk)
    gather_high(4, 2 * blk)
    gather_high(PARTNER, 3 * blk)
    lows, highs = [wall, low_hide(partner)], [wall, high_hide(partner)]
    fold(1, part_of(0), 0, [None, None] + highs, True)
    fold(0, part_of(0), 0, lows, True)
    inner_passes(1)
    fold(1, part_of(1), 0, [None, None] + highs, True)
    inner_passes(2)
    fold(0, part_of(1), 0, lows, True)
    inner_passes(3)

    near_lows, near_highs = [low_hide(near), low_hide(far)], [high_hide(near), high_hide(far)]

    @pl.when(inner == 1)
    def _():
        gather_low(NEAR, 0)
        gather_low(FAR, blk)
        gather_high(NEAR, 2 * blk)
        gather_high(FAR, 3 * blk)

        @both_chunks
        def _(columns):
            fold(1, columns, 0, [None, None] + near_highs)
            fold(0, columns, 0, near_lows)

    outer_passes(0)
    arrived(WIDE, 0)
    arrived(WIDE, 1)
    gather_low(WIDE, 0)

    @both_chunks
    def _(columns):
        fold(1, columns, 0, [None])
        fold(0, columns, 0, [low_hide(wide)])

    outer_passes(1)
    arrived(WIDE, 2)
    arrived(WIDE, 3)
    gather_high(WIDE, blk)

    @both_chunks
    def _(columns):
        fold(1, columns, blk, [high_hide(wide)])

    @pl.when(inner == 0)
    def _():
        arrived(FAR, 0)
        arrived(FAR, 1)
        gather_low(NEAR, 0)
        gather_low(FAR, blk)

        @both_chunks
        def _(columns):
            fold(1, columns, 0, [None, None])
            fold(0, columns, 0, near_lows)

    outer_passes(2)
    outer_passes(3)

    @pl.when(inner == 0)
    def _():
        arrived(FAR, 2)
        arrived(FAR, 3)
        gather_high(NEAR, 2 * blk)
        gather_high(FAR, 3 * blk)

        @both_chunks
        def _(columns):
            fold(1, columns, 2 * blk, near_highs)

    for h in range(heads):
        for b in range(2):
            columns = pl.ds(h * blk, blk)
            o_lat = (acc[b, :, columns] * (1.0 / sum_s[b, :1, columns])).astype(jnp.bfloat16)
            flat[pl.ds(b * blk * heads + h, blk, stride=heads), :] = jnp.dot(
                o_lat.T, wuv[h], preferred_element_type=jnp.float32
            )
    out_ref[...] = flat[...].reshape(out_ref.shape).astype(jnp.bfloat16)
    for copy in own:
        copy.wait_send()

    @pl.when(inner == 1)
    def _():
        for copy in relays + forward + onward:
            copy.wait_send()


def per_device(q_nope, q_rope, c_kv, k_rope, block_pos, w_uk, w_uv):
    rows, heads, nope = q_nope.shape
    blk = rows // 2
    lat = c_kv.shape[1]
    rope = k_rope.shape[1]
    factor = math.log2(math.e) / math.sqrt(nope + rope)
    vmem = pl.BlockSpec(memory_space=pltpu.VMEM)
    anywhere = pl.BlockSpec(memory_space=pltpu.HBM)
    bf16, f32 = jnp.bfloat16, jnp.float32
    return pl.pallas_call(
        functools.partial(attention_kernel, factor),
        out_shape=jax.ShapeDtypeStruct((rows, heads, w_uv.shape[2]), bf16),
        in_specs=[pl.BlockSpec(memory_space=pltpu.SMEM)] + [anywhere] * 6,
        out_specs=vmem,
        scratch_shapes=[
            pltpu.VMEM(c_kv.shape, bf16),
            pltpu.VMEM((rope, rows), bf16),
            pltpu.VMEM(q_nope.shape, bf16),
            pltpu.VMEM((heads, rope, rows), bf16),
            pltpu.VMEM(w_uk.shape, bf16),
            pltpu.VMEM(w_uv.shape, bf16),
            pltpu.VMEM((rows * heads, nope), f32),
            pltpu.VMEM((2, lat + 2 * rope, blk * heads), bf16),
            pltpu.VMEM((5, 9, blk, LANES), bf16),
            pltpu.VMEM((4 * blk, lat + 2 * rope), bf16),
            pltpu.VMEM((lat, 4 * blk), bf16),
            pltpu.VMEM((2, lat, blk * heads), f32),
            pltpu.VMEM((2, 8, blk * heads), f32),
            pltpu.VMEM((2, 8, blk * heads), f32),
            pltpu.VMEM((blk, blk), f32),
            pltpu.SemaphoreType.DMA((6,)),
            pltpu.SemaphoreType.DMA((6, len(PIECES))),
            pltpu.SemaphoreType.DMA((4, len(PIECES))),
        ],
        compiler_params=pltpu.CompilerParams(
            collective_id=0, has_side_effects=True, vmem_limit_bytes=60 * 1024 * 1024
        ),
        cost_estimate=pl.CostEstimate(
            flops=6 * 10**9, bytes_accessed=5 * 10**6, transcendentals=2 * 10**6
        ),
    )(block_pos, c_kv, k_rope.T, q_nope, jnp.transpose(q_rope, (1, 2, 0)), w_uk, w_uv)


def solution(mesh):
    placed = (
        P("ctx", "head", None),
        P("ctx", "head", None),
        P("ctx", None),
        P("ctx", None),
        P(),
        P("head", None, None),
        P("head", None, None),
    )
    return jax.shard_map(
        per_device, mesh=mesh, in_specs=placed, out_specs=P("ctx", "head", None), check_vma=False
    )
```
